32 devices in a mesh: lat: 4 (over x, core), lon: 8 (over z, y).
Axes of the slice: x: 2, y: 2, z: 4, core: 2. Of those that a mesh axis runs over, the one named last changes fastest.
Arguments:
- latent: bfloat16 [32, 2048, 128], P('lat', 'lon'), may hold values from -6 to 6
- head: bfloat16 [128, 32], replicated, may hold values from -0.5 to 0.5
- bias: float32 [32], replicated, may hold values from -3 to 3
- targets: bfloat16 [32, 32, 1024], P(None, 'lat', 'lon'), may hold values from -6 to 6
- margin_cell: int32 [4, 8, 6144], P('lat', 'lon'), may hold values from 0 to 2047
- margin_pixel: int32 [4, 8, 6144], P('lat', 'lon'), may hold values from 0 to 2047, as said below
- margin_weight: float32 [4, 8, 6144], P('lat', 'lon'), may hold values from 0.05 to 1
- live_count: int32 [4, 8], P('lat', 'lon'), may hold values from 2457 to 6144, as said below
Outputs:
- latent_grad: bfloat16 [32, 2048, 128], P('lat', 'lon')
- head_grad: float32 [128, 32], replicated
- bias_grad: float32 [32], replicated
The draws below stay inside these ranges and needn't reach their ends.
Inputs may be any that keep to these rules, and one draw needn't show every extreme that they name: `margin_pixel`: A tile pixel in the device's own band: tile row times (256) plus q, where q - 64 is the column relative to the device's own sector, so q < 64 and q >= 192 are the neighbouring sectors' columns. Both 0 and the largest value occur in every device's list; columns near the frame's edges are covered thinly or not at all. `live_count`: rows at or beyond a device's count are padding and are ignored; in every draw some device has all 6144 rows live.
All inputs are finite; a program needn't handle non-finite values.
Results may differ from the reference program's by a relative error of at most 0.0052.
Values may be sent and summed in bfloat16 or wider, within the bound.
No kernel may reach another device: no remote copies, remote signals or barrier semaphores. Data moves between devices by JAX's collectives and lax.ppermute only.
A program may use at most 64 MiB of HBM per device.

```python
import math
import jax
import jax.numpy as jnp
from jax import lax

LATENT = 128
VARS = 32
CR = 8
CC = 256
TX = 128
TY = 8
REACH = 64
ROWS_DEV = 6144
CYCLES = 32
CYCLE_CELLS = 2048
TILE_ROWS = 32
TILE_COLS = 1024
TOTAL_CELLS = 65536
N_LAT = 4
N_LON = 8


def margin_lists(key):
    base_key = jax.random.fold_in(key, 7)
    key_perm, key_extra, key_row, key_col = jax.random.split(base_key, 4)
    device_count = N_LAT * N_LON
    cell_total = CR * CC
    perms = jax.vmap(lambda sub_key: jax.random.permutation(sub_key, cell_total))(jax.random.split(key_perm, device_count)).astype(jnp.int32)
    extra = jax.random.randint(key_extra, (device_count, ROWS_DEV - cell_total), 0, cell_total, dtype=jnp.int32)
    cell_ids = jnp.concatenate([perms, extra], axis=1)
    cycle = cell_ids // CC
    column = cell_ids % CC
    draw_shape = (device_count, ROWS_DEV)
    row_shift = jax.random.randint(key_row, draw_shape, 0, 2, dtype=jnp.int32)
    tile_row = jnp.minimum(cycle * TY // CR + row_shift, TY - 1)
    col_shift = jax.random.randint(key_col, draw_shape, -REACH, REACH + 1, dtype=jnp.int32)
    tile_col = column * TX // CC + col_shift + REACH
    pixel_ids = tile_row * (TX + 2 * REACH) + tile_col
    cell_ids = cell_ids.at[:, 0].set(cell_total - 1)
    pixel_ids = pixel_ids.at[:, 0].set(TY * (TX + 2 * REACH) - 1)
    pixel_ids = pixel_ids.at[:, 1].set(0)
    return (cell_ids.reshape(N_LAT, N_LON, ROWS_DEV), pixel_ids.reshape(N_LAT, N_LON, ROWS_DEV))


def draw_margin_cell(key, part):
    return margin_lists(key)[0]


def draw_margin_pixel(key, part):
    return margin_lists(key)[1]


def draw_live_count(key, part):
    key_count, key_pick = jax.random.split(jax.random.fold_in(key, 13))
    counts = jax.random.randint(key_count, (N_LAT * N_LON,), 2 * ROWS_DEV // 5, ROWS_DEV + 1, dtype=jnp.int32)
    chosen = jax.random.randint(key_pick, (), 0, N_LAT * N_LON, dtype=jnp.int32)
    counts = counts.at[chosen].set(ROWS_DEV)
    return counts.reshape(N_LAT, N_LON)


def steps_of(own_key, extent, pieces, least, high):
    def one(dim, shards_of):
        heights = jax.random.uniform(jax.random.fold_in(jax.random.fold_in(own_key, 6), dim), (shards_of,), jnp.float32, least / len(pieces), high / len(pieces))
        return jnp.repeat(jnp.exp(heights), extent[dim] // shards_of).reshape((-1,) + (1,) * (len(extent) - dim - 1))

    loudness = one(*pieces[0])
    for cut in pieces[1:]:
        loudness = loudness * one(*cut)
    return loudness


def centred(own_key, shape, width, most, shards=(), kind=jnp.bfloat16):
    result = jax.random.normal(own_key, shape, jnp.float32) * width
    if len(shards) > 0:
        result = steps_of(own_key, shape, shards, -0.22, 0.18) * result
    return jnp.clip(result, min=-most, max=most).astype(kind)


def setup_inputs(seed: int = 0) -> dict:
    seeds = jax.random.split(jax.random.key(seed), 9)
    return {
        "latent": centred(seeds[0], (CYCLES, CYCLE_CELLS, LATENT), 1.0, 6.0, ((0, 4), (1, 8))),
        "head": centred(seeds[1], (LATENT, VARS), LATENT ** -0.5, 0.5),
        "bias": centred(seeds[2], (VARS,), 0.5, 3.0, (), jnp.float32),
        "targets": centred(seeds[3], (VARS, TILE_ROWS, TILE_COLS), 1.0, 6.0, ((1, 4), (2, 8))),
        "margin_cell": draw_margin_cell(jax.random.fold_in(seeds[8], 71), 0),
        "margin_pixel": draw_margin_pixel(jax.random.fold_in(seeds[8], 71), 0),
        "margin_weight": jnp.clip(jnp.exp(math.log(1.0) - 2.9957323 * jax.random.uniform(seeds[6], (N_LAT, N_LON, ROWS_DEV), jnp.float32) ** steps_of(seeds[6], (N_LAT, N_LON, ROWS_DEV), ((0, 4), (1, 8)), -0.2, 0.2)), 0.05, 1.0),
        "live_count": draw_live_count(jax.random.fold_in(seeds[8], 71), 0),
    }


def reference(latent, head, bias, targets, margin_cell, margin_pixel, margin_weight, live_count):
    frame_width = TX + 2 * REACH
    row_index = jnp.arange(ROWS_DEV, dtype=jnp.int32)
    sector = jnp.arange(N_LON, dtype=jnp.int32)[:, None]
    grad_bands = []
    head_total = jnp.zeros((LATENT, VARS), jnp.float32)
    bias_total = jnp.zeros((VARS,), jnp.float32)
    for band_index in range(N_LAT):
        band_latent = latent[band_index * CR:(band_index + 1) * CR].reshape(CR * CYCLE_CELLS, LATENT)
        predicted = (jnp.dot(band_latent, head, preferred_element_type=jnp.float32) + bias).astype(jnp.bfloat16)
        local_cell = margin_cell[band_index]
        local_pixel = margin_pixel[band_index]
        cell_index = local_cell // CC * CYCLE_CELLS + sector * CC + local_cell % CC
        pixel_row = local_pixel // frame_width
        pixel_col = local_pixel % frame_width
        pixel_index = pixel_row * TILE_COLS + (sector * TX + pixel_col - REACH) % TILE_COLS
        live_weight = jnp.where(row_index[None, :] < live_count[band_index][:, None], margin_weight[band_index], jnp.float32(0.0))
        cell_flat = cell_index.reshape(-1).astype(jnp.int32)
        pixel_flat = pixel_index.reshape(-1).astype(jnp.int32)
        weight_flat = live_weight.reshape(-1)
        contribution = predicted[cell_flat].astype(jnp.float32) * weight_flat[:, None]
        tiles = jax.ops.segment_sum(contribution, pixel_flat, num_segments=TY * TILE_COLS)
        band_target = targets[:, band_index * TY:(band_index + 1) * TY, :].reshape(VARS, TY * TILE_COLS).T.astype(jnp.float32)
        misfit = tiles - band_target
        backward = misfit[pixel_flat] * weight_flat[:, None]
        cell_misfit = jax.ops.segment_sum(backward, cell_flat, num_segments=CR * CYCLE_CELLS).astype(jnp.bfloat16)
        band_grad = jnp.dot(cell_misfit, head.T, preferred_element_type=jnp.float32).astype(jnp.bfloat16)
        grad_bands.append(band_grad.reshape(CR, CYCLE_CELLS, LATENT))
        head_total = head_total + lax.dot_general(band_latent, cell_misfit, (((0,), (0,)), ((), ())), preferred_element_type=jnp.float32)
        bias_total = bias_total + lax.optimization_barrier(jnp.sum(cell_misfit.astype(jnp.float32), axis=0))
    grad_scale = 1.0 / math.sqrt(TOTAL_CELLS)
    return (jnp.concatenate(grad_bands, axis=0), head_total * grad_scale, bias_total * grad_scale)
```

```python
import functools
import math

import jax
import jax.numpy as jnp
from jax import lax
from jax.experimental import pallas as pl
from jax.experimental.pallas import tpu as pltpu
from jax.sharding import PartitionSpec as P

BF16 = jnp.bfloat16
F32 = jnp.float32
NN = (((1,), (0,)), ((), ()))
NT = (((1,), (1,)), ((), ()))
TN = (((0,), (0,)), ((), ()))


def dot(a, b, dims):
    return lax.dot_general(a, b, dims, preferred_element_type=F32)


def low_one_hot(ids, low):
    rows = lax.broadcasted_iota(jnp.int32, (low, ids.shape[1]), 0)
    return jnp.where(rows == (ids & (low - 1)), 1.0, 0.0).astype(BF16)


def pick_group(stacked, high, groups):
    size = stacked.shape[0] // groups
    picked = stacked[:size]
    for g in range(1, groups):
        picked = jnp.where(high == g, stacked[g * size : (g + 1) * size], picked)
    return picked


def spread_groups(values, high, groups):
    return jnp.concatenate(
        [jnp.where(high == g, values, 0.0).astype(BF16) for g in range(groups)], axis=0
    )


def live_weights(weight_ref, live, start, span):
    index = lax.broadcasted_iota(jnp.int32, (1, span), 1) + start
    return jnp.where(index < live, weight_ref[:, pl.ds(start, span)], 0.0)


def forward_kernel(
    span,
    live_ref,
    latent_ref,
    head_ref,
    bias_ref,
    targets_ref,
    cell_ref,
    pixel_ref,
    weight_ref,
    frame_ref,
    west_ref,
    east_ref,
    predicted,
    wide_targets,
):
    cycles, low_cells, _ = latent_ref.shape
    variables, tile_rows, tile_cols = targets_ref.shape
    frame_width = 2 * tile_cols
    rim = tile_cols // 2
    live = live_ref[0, 0]
    eye = lax.broadcasted_iota(jnp.int32, (variables, variables), 0) == lax.broadcasted_iota(
        jnp.int32, (variables, variables), 1
    )
    bias = jnp.sum(jnp.where(eye, bias_ref[...], 0.0), axis=1, keepdims=True)
    head_t = head_ref[...].astype(F32).T.astype(BF16)
    for c in range(cycles):
        predicted[c * variables : (c + 1) * variables, :] = (
            dot(head_t, latent_ref[c], NT) + bias
        ).astype(BF16)
    wide_targets[...] = targets_ref[...].astype(F32)
    frame_ref[...] = jnp.zeros_like(frame_ref)
    for start in range(0, cell_ref.shape[1], span):
        cell = cell_ref[:, pl.ds(start, span)]
        pixel = pixel_ref[:, pl.ds(start, span)]
        weight = live_weights(weight_ref, live, start, span)
        gathered = dot(predicted[...], low_one_hot(cell, low_cells), NN)
        share = pick_group(gathered, cell // low_cells, cycles) * weight
        frame_ref[...] += dot(
            spread_groups(share, pixel // frame_width, tile_rows),
            low_one_hot(pixel, frame_width),
            NT,
        )
    for t in range(tile_rows):
        rows = slice(t * variables, (t + 1) * variables)
        frame_ref[rows, rim : rim + tile_cols] -= wide_targets[:, t, :]
    west_ref[...] = frame_ref[:, :tile_cols].astype(BF16)
    east_ref[...] = frame_ref[:, tile_cols:].astype(BF16)


def backward_kernel(
    span,
    tile_rows,
    live_ref,
    frame_ref,
    from_west_ref,
    from_east_ref,
    latent_ref,
    head_ref,
    cell_ref,
    pixel_ref,
    weight_ref,
    latent_grad_ref,
    part_ref,
    misfit,
    totals,
):
    cycles, low_cells, _ = latent_ref.shape
    variables = head_ref.shape[1]
    frame_width = frame_ref.shape[1]
    half = frame_width // 2
    live = live_ref[0, 0]
    misfit[:, :half] = (frame_ref[:, :half] + from_west_ref[...].astype(F32)).astype(BF16)
    misfit[:, half:] = (frame_ref[:, half:] + from_east_ref[...].astype(F32)).astype(BF16)
    totals[...] = jnp.zeros_like(totals)
    for start in range(0, cell_ref.shape[1], span):
        cell = cell_ref[:, pl.ds(start, span)]
        pixel = pixel_ref[:, pl.ds(start, span)]
        weight = live_weights(weight_ref, live, start, span)
        gathered = dot(misfit[...], low_one_hot(pixel, frame_width), NN)
        share = pick_group(gathered, pixel // frame_width, tile_rows) * weight
        totals[...] += dot(
            spread_groups(share, cell // low_cells, cycles), low_one_hot(cell, low_cells), NT
        )
    head_t = head_ref[...].astype(F32).T.astype(BF16)
    head_part = jnp.zeros((variables, latent_ref.shape[2]), F32)
    bias_part = jnp.zeros((variables, 1), F32)
    for c in range(cycles):
        cell_misfit = totals[c * variables : (c + 1) * variables, :].astype(BF16)
        wide = cell_misfit.astype(F32)
        head_part += dot(cell_misfit, latent_ref[c], NN)
        bias_part += jnp.sum(wide, axis=1, keepdims=True)
        latent_grad_ref[c] = dot(wide.T.astype(BF16), head_t, NN).astype(BF16)
    part_ref[...] = jnp.zeros_like(part_ref)
    part_ref[:variables, :] = head_part
    eye = lax.broadcasted_iota(jnp.int32, (variables, variables), 0) == lax.broadcasted_iota(
        jnp.int32, (variables, variables), 1
    )
    part_ref[variables : variables + 1, :variables] = jnp.sum(
        jnp.where(eye, bias_part, 0.0), axis=0, keepdims=True
    )


def sum_over(value, axis):
    devices = lax.axis_size(axis)
    if devices & (devices - 1):
        return lax.psum(value, axis)
    step = 1
    while step < devices:
        value = value + lax.ppermute(value, axis, [(i, i ^ step) for i in range(devices)])
        step *= 2
    return value


def from_behind(shard, axis, by):
    devices = lax.axis_size(axis)
    return lax.ppermute(shard, axis, [(i, (i + by) % devices) for i in range(devices)])


def per_device(latent, head, bias, targets, margin_cell, margin_pixel, margin_weight, live_count):
    cycles, low_cells, width = latent.shape
    variables, tile_rows, tile_cols = targets.shape
    frame_shape = (tile_rows * variables, 2 * tile_cols)
    half_shape = (tile_rows * variables, tile_cols)
    cell_shape = (cycles * variables, low_cells)
    cell = margin_cell.reshape(1, -1)
    pixel = margin_pixel.reshape(1, -1)
    weight = margin_weight.reshape(1, -1)
    span = min(512, cell.shape[1])
    smem = pl.BlockSpec(memory_space=pltpu.SMEM)
    vmem = pl.BlockSpec(memory_space=pltpu.VMEM)
    params = pltpu.CompilerParams(vmem_limit_bytes=32 * 1024 * 1024)
    frame, west, east = pl.pallas_call(
        functools.partial(forward_kernel, span),
        out_shape=(
            jax.ShapeDtypeStruct(frame_shape, F32),
            jax.ShapeDtypeStruct(half_shape, BF16),
            jax.ShapeDtypeStruct(half_shape, BF16),
        ),
        in_specs=[smem] + [vmem] * 7,
        out_specs=(vmem, vmem, vmem),
        scratch_shapes=[
            pltpu.VMEM(cell_shape, BF16),
            pltpu.VMEM((variables, tile_rows, tile_cols), F32),
        ],
        compiler_params=params,
        name="forward",
    )(live_count, latent, head, bias.reshape(1, -1), targets, cell, pixel, weight)
    from_west = from_behind(east, "lon", 1)
    from_east = from_behind(west, "lon", -1)
    latent_grad, part = pl.pallas_call(
        functools.partial(backward_kernel, span, tile_rows),
        out_shape=(
            jax.ShapeDtypeStruct(latent.shape, BF16),
            jax.ShapeDtypeStruct((variables + 8, width), F32),
        ),
        in_specs=[smem] + [vmem] * 8,
        out_specs=(vmem, vmem),
        scratch_shapes=[
            pltpu.VMEM(frame_shape, BF16),
            pltpu.VMEM(cell_shape, F32),
        ],
        compiler_params=params,
        name="backward",
    )(live_count, frame, from_west, from_east, latent, head, cell, pixel, weight)
    total = sum_over(sum_over(part, "lat"), "lon")
    cell_total = cycles * low_cells * lax.axis_size("lat") * lax.axis_size("lon")
    total = total * (1.0 / math.sqrt(cell_total))
    return latent_grad, total[:variables].T, total[variables, :variables]


def solution(mesh):
    in_specs = (
        P("lat", "lon", None),
        P(),
        P(),
        P(None, "lat", "lon"),
        P("lat", "lon", None),
        P("lat", "lon", None),
        P("lat", "lon", None),
        P("lat", "lon"),
    )
    out_specs = (P("lat", "lon", None), P(), P())
    return jax.shard_map(
        per_device, mesh=mesh, in_specs=in_specs, out_specs=out_specs, check_vma=False
    )
```

```python
import functools
import math

import jax
import jax.numpy as jnp
from jax import lax
from jax.experimental import pallas as pl
from jax.experimental.pallas import tpu as pltpu
from jax.sharding import PartitionSpec as P

BF16 = jnp.bfloat16
F32 = jnp.float32
NN = (((1,), (0,)), ((), ()))
NT = (((1,), (1,)), ((), ()))


def dot(a, b, dims):
    return lax.dot_general(a, b, dims, preferred_element_type=F32)


def low_one_hot(ids, low):
    rows = lax.broadcasted_iota(jnp.int32, (low, ids.shape[1]), 0)
    return jnp.where(rows == (ids & (low - 1)), 1.0, 0.0).astype(BF16)


def pick_group(stacked, high, groups):
    size = stacked.shape[0] // groups
    picked = stacked[:size]
    for g in range(1, groups):
        picked = jnp.where(high == g, stacked[g * size : (g + 1) * size], picked)
    return picked


def spread_groups(values, high, groups):
    return jnp.concatenate(
        [jnp.where(high == g, values, 0.0).astype(BF16) for g in range(groups)], axis=0
    )


def eye(size):
    rows = lax.broadcasted_iota(jnp.int32, (size, size), 0)
    return rows == lax.broadcasted_iota(jnp.int32, (size, size), 1)


def forward_kernel(
    span,
    live_ref,
    latent_hbm,
    head_hbm,
    bias_hbm,
    targets_hbm,
    cell_hbm,
    pixel_hbm,
    weight_hbm,
    frame_ref,
    west_ref,
    east_ref,
    latent_ref,
    head_ref,
    cell_ref,
    pixel_ref,
    weight_ref,
    bias_ref,
    targets_ref,
    predicted,
    wide_targets,
    sems,
):
    copies = [
        pltpu.make_async_copy(source, target, sems.at[i])
        for i, (source, target) in enumerate(
            (
                (head_hbm, head_ref),
                (bias_hbm, bias_ref),
                (latent_hbm, latent_ref),
                (cell_hbm, cell_ref),
                (pixel_hbm, pixel_ref),
                (weight_hbm, weight_ref),
                (targets_hbm, targets_ref),
            )
        )
    ]
    for copy in copies:
        copy.start()
    cycles, low_cells, _ = latent_ref.shape
    variables, tile_rows, tile_cols = targets_ref.shape
    frame_width = 2 * tile_cols
    rim = tile_cols // 2
    frame_ref[...] = jnp.zeros_like(frame_ref)
    for copy in copies[:3]:
        copy.wait()
    bias = jnp.sum(jnp.where(eye(variables), bias_ref[...], 0.0), axis=1, keepdims=True)
    for c in range(cycles):
        predicted[c * variables : (c + 1) * variables, :] = (
            dot(head_ref[...], latent_ref[c], NT) + bias
        ).astype(BF16)
    for copy in copies[3:]:
        copy.wait()
    rows = lax.broadcasted_iota(jnp.int32, weight_ref.shape, 1)
    weight_ref[...] = jnp.where(rows < live_ref[0, 0], weight_ref[...], 0.0)
    wide_targets[...] = targets_ref[...].astype(F32)
    for start in range(0, cell_ref.shape[1], span):
        cell = cell_ref[:, pl.ds(start, span)]
        pixel = pixel_ref[:, pl.ds(start, span)]
        weight = weight_ref[:, pl.ds(start, span)]
        gathered = dot(predicted[...], low_one_hot(cell, low_cells), NN)
        share = pick_group(gathered, cell // low_cells, cycles) * weight
        frame_ref[...] += dot(
            spread_groups(share, pixel // frame_width, tile_rows),
            low_one_hot(pixel, frame_width),
            NT,
        )
    for t in range(tile_rows):
        rows = slice(t * variables, (t + 1) * variables)
        frame_ref[rows, rim : rim + tile_cols] -= wide_targets[:, t, :]
    west_ref[...] = frame_ref[:, :tile_cols].astype(BF16)
    east_ref[...] = frame_ref[:, tile_cols:].astype(BF16)


def backward_kernel(
    span,
    tile_rows,
    frame_ref,
    from_west_ref,
    from_east_ref,
    latent_ref,
    cell_ref,
    pixel_ref,
    weight_ref,
    cell_misfit_ref,
    part_ref,
    misfit,
    totals,
):
    cycles, low_cells, _ = latent_ref.shape
    frame_rows, frame_width = frame_ref.shape
    variables = frame_rows // tile_rows
    half = frame_width // 2
    misfit[:, :half] = (frame_ref[:, :half] + from_west_ref[...].astype(F32)).astype(BF16)
    misfit[:, half:] = (frame_ref[:, half:] + from_east_ref[...].astype(F32)).astype(BF16)
    totals[...] = jnp.zeros_like(totals)
    for start in range(0, cell_ref.shape[1], span):
        cell = cell_ref[:, pl.ds(start, span)]
        pixel = pixel_ref[:, pl.ds(start, span)]
        weight = weight_ref[:, pl.ds(start, span)]
        gathered = dot(misfit[...], low_one_hot(pixel, frame_width), NN)
        share = pick_group(gathered, pixel // frame_width, tile_rows) * weight
        totals[...] += dot(
            spread_groups(share, cell // low_cells, cycles), low_one_hot(cell, low_cells), NT
        )
    head_part = jnp.zeros((variables, latent_ref.shape[2]), F32)
    bias_part = jnp.zeros((variables, 1), F32)
    for c in range(cycles):
        rows = slice(c * variables, (c + 1) * variables)
        cell_misfit = totals[rows, :].astype(BF16)
        cell_misfit_ref[rows, :] = cell_misfit
        head_part += dot(cell_misfit, latent_ref[c], NN)
        bias_part += jnp.sum(cell_misfit.astype(F32), axis=1, keepdims=True)
    part_ref[...] = jnp.zeros_like(part_ref)
    part_ref[:variables, :] = head_part
    part_ref[variables : variables + 1, :variables] = jnp.sum(
        jnp.where(eye(variables), bias_part, 0.0), axis=0, keepdims=True
    )


def latent_kernel(cell_misfit_ref, head_ref, latent_grad_ref):
    variables = head_ref.shape[0]
    for c in range(latent_grad_ref.shape[0]):
        rows = slice(c * variables, (c + 1) * variables)
        wide = cell_misfit_ref[rows, :].astype(F32)
        latent_grad_ref[c] = dot(wide.T.astype(BF16), head_ref[...], NN).astype(BF16)


def finish_kernel(scale, mine_ref, theirs_ref, head_grad_ref, bias_grad_ref):
    variables = head_grad_ref.shape[0]
    head_grad_ref[...] = (mine_ref[:variables, :] + theirs_ref[:variables, :]) * scale
    last = slice(variables, variables + 1)
    bias_grad_ref[...] = (mine_ref[last, :variables] + theirs_ref[last, :variables]) * scale


def sum_rounds(lat, lon):
    rounds = []
    for size, make in ((lat, lambda s: (s, 0)), (lon, lambda s: (1 if lat > 1 else 0, s))):
        steps = [1 << k for k in range(size.bit_length() - 1)]
        while steps:
            pair, steps = steps[:2], steps[2:]
            rounds.append([make(s) for s in pair + ([pair[0] ^ pair[1]] if len(pair) > 1 else [])])
    return rounds


def add_pairs(values):
    while len(values) > 1:
        values = [values[i] + values[i + 1] for i in range(0, len(values), 2)]
    return values[0]


def sum_but_last(value):
    lat, lon = lax.axis_size("lat"), lax.axis_size("lon")

    def swap(shard, flip):
        pairs = [
            (i * lon + j, (i ^ flip[0]) * lon + (j ^ flip[1])) for i in range(lat) for j in range(lon)
        ]
        return lax.ppermute(shard, ("lat", "lon"), pairs)

    if lat & (lat - 1) or lon & (lon - 1) or lat * lon == 1:
        return lax.psum(value, ("lat", "lon")), jnp.zeros_like(value)
    rounds = sum_rounds(lat, lon)
    for flips in rounds[:-1]:
        value = add_pairs([value] + [swap(value, flip) for flip in flips])
    last = [value] + [swap(value, flip) for flip in rounds[-1]]
    return add_pairs(last[: len(last) // 2]), add_pairs(last[len(last) // 2 :])


def from_behind(shard, axis, by):
    devices = lax.axis_size(axis)
    return lax.ppermute(shard, axis, [(i, (i + by) % devices) for i in range(devices)])


def per_device(latent, head, bias, targets, margin_cell, margin_pixel, margin_weight, live_count):
    cycles, low_cells, width = latent.shape
    variables, tile_rows, tile_cols = targets.shape
    frame_shape = (tile_rows * variables, 2 * tile_cols)
    half_shape = (tile_rows * variables, tile_cols)
    cell_shape = (cycles * variables, low_cells)
    cell = margin_cell.reshape(1, -1)
    pixel = margin_pixel.reshape(1, -1)
    weight = margin_weight.reshape(1, -1)
    span = min(512, cell.shape[1])
    hbm = pl.BlockSpec(memory_space=pltpu.HBM)
    vmem = pl.BlockSpec(memory_space=pltpu.VMEM)
    params = pltpu.CompilerParams(vmem_limit_bytes=24 * 1024 * 1024)
    frame, west, east, latent, head_t, cell, pixel, weight = pl.pallas_call(
        functools.partial(forward_kernel, span),
        out_shape=(
            jax.ShapeDtypeStruct(frame_shape, F32),
            jax.ShapeDtypeStruct(half_shape, BF16),
            jax.ShapeDtypeStruct(half_shape, BF16),
            jax.ShapeDtypeStruct(latent.shape, BF16),
            jax.ShapeDtypeStruct((variables, width), BF16),
            jax.ShapeDtypeStruct(cell.shape, jnp.int32),
            jax.ShapeDtypeStruct(cell.shape, jnp.int32),
            jax.ShapeDtypeStruct(cell.shape, F32),
        ),
        in_specs=[pl.BlockSpec(memory_space=pltpu.SMEM)] + [hbm] * 7,
        out_specs=[vmem] * 8,
        scratch_shapes=[
            pltpu.VMEM((1, variables), F32),
            pltpu.VMEM(targets.shape, BF16),
            pltpu.VMEM(cell_shape, BF16),
            pltpu.VMEM((variables, tile_rows, tile_cols), F32),
            pltpu.SemaphoreType.DMA((7,)),
        ],
        compiler_params=params,
        name="forward",
    )(
        live_count,
        *(
            pltpu.with_memory_space_constraint(array, pltpu.HBM)
            for array in (latent, head.T, bias.reshape(1, -1), targets, cell, pixel, weight)
        ),
    )
    from_west = from_behind(east, "lon", 1)
    from_east = from_behind(west, "lon", -1)
    cell_misfit, part = pl.pallas_call(
        functools.partial(backward_kernel, span, tile_rows),
        out_shape=(
            jax.ShapeDtypeStruct(cell_shape, BF16),
            jax.ShapeDtypeStruct((variables + 8, width), F32),
        ),
        in_specs=[vmem] * 7,
        out_specs=(vmem, vmem),
        scratch_shapes=[
            pltpu.VMEM(frame_shape, BF16),
            pltpu.VMEM(cell_shape, F32),
        ],
        compiler_params=params,
        name="backward",
    )(frame, from_west, from_east, latent, cell, pixel, weight)
    latent_grad = pl.pallas_call(
        latent_kernel,
        out_shape=jax.ShapeDtypeStruct(latent.shape, BF16),
        in_specs=[vmem, vmem],
        out_specs=vmem,
        compiler_params=params,
        cost_estimate=pl.CostEstimate(
            flops=2 * cycles * low_cells * width * variables,
            bytes_accessed=2 * cycles * low_cells * width,
            transcendentals=0,
        ),
        name="latent_gradient",
    )(cell_misfit, head_t)
    mine, theirs = sum_but_last(part)
    cell_total = cycles * low_cells * lax.axis_size("lat") * lax.axis_size("lon")
    head_grad, bias_grad = pl.pallas_call(
        functools.partial(finish_kernel, 1.0 / math.sqrt(cell_total)),
        out_shape=(
            jax.ShapeDtypeStruct((variables, width), F32),
            jax.ShapeDtypeStruct((1, variables), F32),
        ),
        in_specs=[vmem, vmem],
        out_specs=(vmem, vmem),
        name="finish",
    )(mine, theirs)
    return latent_grad, head_grad.T, bias_grad.reshape(variables)


def solution(mesh):
    in_specs = (
        P("lat", "lon", None),
        P(),
        P(),
        P(None, "lat", "lon"),
        P("lat", "lon", None),
        P("lat", "lon", None),
        P("lat", "lon", None),
        P("lat", "lon"),
    )
    out_specs = (P("lat", "lon", None), P(), P())
    return jax.shard_map(
        per_device, mesh=mesh, in_specs=in_specs, out_specs=out_specs, check_vma=False
    )
```

```python
import functools
import math

import jax
import jax.numpy as jnp
from jax import lax
from jax.experimental import pallas as pl
from jax.experimental.pallas import tpu as pltpu
from jax.sharding import PartitionSpec as P

BF16 = jnp.bfloat16
F32 = jnp.float32
NN = (((1,), (0,)), ((), ()))
NT = (((1,), (1,)), ((), ()))


def dot(a, b, dims):
    return lax.dot_general(a, b, dims, preferred_element_type=F32)


def low_one_hot(ids, low):
    rows = lax.broadcasted_iota(jnp.int32, (low, ids.shape[1]), 0).astype(BF16)
    return jnp.where(rows == (ids & (low - 1)).astype(BF16), jnp.ones((), BF16), jnp.zeros((), BF16))


def pick_group(stacked, high, groups):
    size = stacked.shape[0] // groups
    picked = stacked[:size]
    for g in range(1, groups):
        picked = jnp.where(high == g, stacked[g * size : (g + 1) * size], picked)
    return picked


def spread_groups(values, high, groups):
    narrow = values.astype(BF16)
    return jnp.concatenate(
        [narrow * jnp.where(high == g, 1.0, 0.0).astype(BF16) for g in range(groups)], axis=0
    )


def eye(size):
    rows = lax.broadcasted_iota(jnp.int32, (size, size), 0)
    return rows == lax.broadcasted_iota(jnp.int32, (size, size), 1)


def forward_kernel(
    span,
    live_ref,
    latent_hbm,
    head_hbm,
    bias_hbm,
    targets_hbm,
    cell_hbm,
    pixel_hbm,
    weight_hbm,
    frame_ref,
    west_ref,
    east_ref,
    latent_ref,
    head_ref,
    cell_ref,
    pixel_ref,
    weight_ref,
    bias_ref,
    targets_ref,
    predicted,
    wide_targets,
    sems,
):
    copies = [
        pltpu.make_async_copy(source, target, sems.at[i])
        for i, (source, target) in enumerate(
            (
                (head_hbm, head_ref),
                (bias_hbm, bias_ref),
                (latent_hbm, latent_ref),
                (cell_hbm, cell_ref),
                (pixel_hbm, pixel_ref),
                (weight_hbm, weight_ref),
                (targets_hbm, targets_ref),
            )
        )
    ]
    for copy in copies:
        copy.start()
    cycles, low_cells, _ = latent_ref.shape
    variables, tile_rows, tile_cols = targets_ref.shape
    frame_width = 2 * tile_cols
    rim = tile_cols // 2
    frame_ref[...] = jnp.zeros_like(frame_ref)
    for copy in copies[:3]:
        copy.wait()
    bias = jnp.sum(jnp.where(eye(variables), bias_ref[...], 0.0), axis=1, keepdims=True)
    for c in range(cycles):
        predicted[c * variables : (c + 1) * variables, :] = (
            dot(head_ref[...], latent_ref[c], NT) + bias
        ).astype(BF16)
    for copy in copies[3:]:
        copy.wait()
    rows = lax.broadcasted_iota(jnp.int32, weight_ref.shape, 1)
    weight_ref[...] = jnp.where(rows < live_ref[0, 0], weight_ref[...], 0.0)
    wide_targets[...] = targets_ref[...].astype(F32)
    for start in range(0, cell_ref.shape[1], span):
        cell = cell_ref[:, pl.ds(start, span)]
        pixel = pixel_ref[:, pl.ds(start, span)]
        weight = weight_ref[:, pl.ds(start, span)]
        gathered = dot(predicted[...], low_one_hot(cell, low_cells), NN)
        share = pick_group(gathered, cell // low_cells, cycles) * weight
        frame_ref[...] += dot(
            spread_groups(share, pixel // frame_width, tile_rows),
            low_one_hot(pixel, frame_width),
            NT,
        )
    for t in range(tile_rows):
        rows = slice(t * variables, (t + 1) * variables)
        frame_ref[rows, rim : rim + tile_cols] -= wide_targets[:, t, :]
    west_ref[...] = frame_ref[:, :tile_cols].astype(BF16)
    east_ref[...] = frame_ref[:, tile_cols:].astype(BF16)


def backward_kernel(
    span,
    tile_rows,
    frame_ref,
    from_west_ref,
    from_east_ref,
    latent_ref,
    cell_ref,
    pixel_ref,
    weight_ref,
    cell_misfit_ref,
    part_ref,
    misfit,
    totals,
):
    cycles, low_cells, _ = latent_ref.shape
    frame_rows, frame_width = frame_ref.shape
    variables = frame_rows // tile_rows
    half = frame_width // 2
    misfit[:, :half] = (frame_ref[:, :half] + from_west_ref[...].astype(F32)).astype(BF16)
    misfit[:, half:] = (frame_ref[:, half:] + from_east_ref[...].astype(F32)).astype(BF16)
    totals[...] = jnp.zeros_like(totals)
    for start in range(0, cell_ref.shape[1], span):
        cell = cell_ref[:, pl.ds(start, span)]
        pixel = pixel_ref[:, pl.ds(start, span)]
        weight = weight_ref[:, pl.ds(start, span)]
        gathered = dot(misfit[...], low_one_hot(pixel, frame_width), NN)
        share = pick_group(gathered, pixel // frame_width, tile_rows) * weight
        totals[...] += dot(
            spread_groups(share, cell // low_cells, cycles), low_one_hot(cell, low_cells), NT
        )
    head_part = jnp.zeros((variables, latent_ref.shape[2]), F32)
    bias_part = jnp.zeros((variables, 1), F32)
    for c in range(cycles):
        rows = slice(c * variables, (c + 1) * variables)
        cell_misfit = totals[rows, :].astype(BF16)
        cell_misfit_ref[rows, :] = cell_misfit
        head_part += dot(cell_misfit, latent_ref[c], NN)
        bias_part += jnp.sum(cell_misfit.astype(F32), axis=1, keepdims=True)
    part_ref[...] = jnp.zeros_like(part_ref)
    part_ref[:variables, :] = head_part
    part_ref[variables : variables + 1, :variables] = jnp.sum(
        jnp.where(eye(variables), bias_part, 0.0), axis=0, keepdims=True
    )


def latent_kernel(cell_misfit_ref, head_ref, latent_grad_ref):
    variables = head_ref.shape[0]
    for c in range(latent_grad_ref.shape[0]):
        rows = slice(c * variables, (c + 1) * variables)
        wide = cell_misfit_ref[rows, :].astype(F32)
        latent_grad_ref[c] = dot(wide.T.astype(BF16), head_ref[...], NN).astype(BF16)


def finish_kernel(scale, mine_ref, theirs_ref, head_grad_ref, bias_grad_ref):
    variables = head_grad_ref.shape[0]
    head_grad_ref[...] = (mine_ref[:variables, :] + theirs_ref[:variables, :]) * scale
    last = slice(variables, variables + 1)
    bias_grad_ref[...] = (mine_ref[last, :variables] + theirs_ref[last, :variables]) * scale


def sum_rounds(lat, lon):
    rounds = []
    for size, make in ((lat, lambda s: (s, 0)), (lon, lambda s: (1 if lat > 1 else 0, s))):
        steps = [1 << k for k in range(size.bit_length() - 1)]
        while steps:
            pair, steps = steps[:2], steps[2:]
            rounds.append([make(s) for s in pair + ([pair[0] ^ pair[1]] if len(pair) > 1 else [])])
    return rounds


def add_pairs(values):
    while len(values) > 1:
        values = [values[i] + values[i + 1] for i in range(0, len(values), 2)]
    return values[0]


def sum_but_last(value):
    lat, lon = lax.axis_size("lat"), lax.axis_size("lon")

    def swap(shard, flip):
        pairs = [
            (i * lon + j, (i ^ flip[0]) * lon + (j ^ flip[1])) for i in range(lat) for j in range(lon)
        ]
        return lax.ppermute(shard, ("lat", "lon"), pairs)

    if lat & (lat - 1) or lon & (lon - 1) or lat * lon == 1:
        return lax.psum(value, ("lat", "lon")), jnp.zeros_like(value)
    rounds = sum_rounds(lat, lon)
    for flips in rounds[:-1]:
        value = add_pairs([value] + [swap(value, flip) for flip in flips])
    last = [value] + [swap(value, flip) for flip in rounds[-1]]
    return add_pairs(last[: len(last) // 2]), add_pairs(last[len(last) // 2 :])


def from_behind(shard, axis, by):
    devices = lax.axis_size(axis)
    return lax.ppermute(shard, axis, [(i, (i + by) % devices) for i in range(devices)])


def per_device(latent, head, bias, targets, margin_cell, margin_pixel, margin_weight, live_count):
    cycles, low_cells, width = latent.shape
    variables, tile_rows, tile_cols = targets.shape
    frame_shape = (tile_rows * variables, 2 * tile_cols)
    half_shape = (tile_rows * variables, tile_cols)
    cell_shape = (cycles * variables, low_cells)
    cell = margin_cell.reshape(1, -1)
    pixel = margin_pixel.reshape(1, -1)
    weight = margin_weight.reshape(1, -1)
    span = min(1024, cell.shape[1])
    hbm = pl.BlockSpec(memory_space=pltpu.HBM)
    vmem = pl.BlockSpec(memory_space=pltpu.VMEM)
    params = pltpu.CompilerParams(vmem_limit_bytes=24 * 1024 * 1024)
    frame, west, east, latent, head_t, cell, pixel, weight = pl.pallas_call(
        functools.partial(forward_kernel, span),
        out_shape=(
            jax.ShapeDtypeStruct(frame_shape, F32),
            jax.ShapeDtypeStruct(half_shape, BF16),
            jax.ShapeDtypeStruct(half_shape, BF16),
            jax.ShapeDtypeStruct(latent.shape, BF16),
            jax.ShapeDtypeStruct((variables, width), BF16),
            jax.ShapeDtypeStruct(cell.shape, jnp.int32),
            jax.ShapeDtypeStruct(cell.shape, jnp.int32),
            jax.ShapeDtypeStruct(cell.shape, F32),
        ),
        in_specs=[pl.BlockSpec(memory_space=pltpu.SMEM)] + [hbm] * 7,
        out_specs=[vmem] * 8,
        scratch_shapes=[
            pltpu.VMEM((1, variables), F32),
            pltpu.VMEM(targets.shape, BF16),
            pltpu.VMEM(cell_shape, BF16),
            pltpu.VMEM((variables, tile_rows, tile_cols), F32),
            pltpu.SemaphoreType.DMA((7,)),
        ],
        compiler_params=params,
        name="forward",
    )(
        live_count,
        *(
            pltpu.with_memory_space_constraint(array, pltpu.HBM)
            for array in (latent, head.T, bias.reshape(1, -1), targets, cell, pixel, weight)
        ),
    )
    from_west = from_behind(east, "lon", 1)
    from_east = from_behind(west, "lon", -1)
    cell_misfit, part = pl.pallas_call(
        functools.partial(backward_kernel, span, tile_rows),
        out_shape=(
            jax.ShapeDtypeStruct(cell_shape, BF16),
            jax.ShapeDtypeStruct((variables + 8, width), F32),
        ),
        in_specs=[vmem] * 7,
        out_specs=(vmem, vmem),
        scratch_shapes=[
            pltpu.VMEM(frame_shape, BF16),
            pltpu.VMEM(cell_shape, F32),
        ],
        compiler_params=params,
        name="backward",
    )(frame, from_west, from_east, latent, cell, pixel, weight)
    latent_grad = pl.pallas_call(
        latent_kernel,
        out_shape=jax.ShapeDtypeStruct(latent.shape, BF16),
        in_specs=[vmem, vmem],
        out_specs=vmem,
        compiler_params=params,
        cost_estimate=pl.CostEstimate(
            flops=2 * cycles * low_cells * width * variables,
            bytes_accessed=2 * cycles * low_cells * width,
            transcendentals=0,
        ),
        name="latent_gradient",
    )(cell_misfit, head_t)
    mine, theirs = sum_but_last(part)
    cell_total = cycles * low_cells * lax.axis_size("lat") * lax.axis_size("lon")
    head_grad, bias_grad = pl.pallas_call(
        functools.partial(finish_kernel, 1.0 / math.sqrt(cell_total)),
        out_shape=(
            jax.ShapeDtypeStruct((variables, width), F32),
            jax.ShapeDtypeStruct((1, variables), F32),
        ),
        in_specs=[vmem, vmem],
        out_specs=(vmem, vmem),
        compiler_params=pltpu.CompilerParams(vmem_limit_bytes=1024 * 1024),
        name="finish",
    )(mine, theirs)
    return latent_grad, head_grad.T, bias_grad.reshape(variables)


def solution(mesh):
    in_specs = (
        P("lat", "lon", None),
        P(),
        P(),
        P(None, "lat", "lon"),
        P("lat", "lon", None),
        P("lat", "lon", None),
        P("lat", "lon", None),
        P("lat", "lon"),
    )
    out_specs = (P("lat", "lon", None), P(), P())
    return jax.shard_map(
        per_device, mesh=mesh, in_specs=in_specs, out_specs=out_specs, check_vma=False
    )
```

```python
import functools
import math

import jax
import jax.numpy as jnp
from jax import lax
from jax.experimental import pallas as pl
from jax.experimental.pallas import tpu as pltpu
from jax.sharding import PartitionSpec as P

BF16 = jnp.bfloat16
F32 = jnp.float32
NN = (((1,), (0,)), ((), ()))
NT = (((1,), (1,)), ((), ()))


def dot(a, b, dims):
    return lax.dot_general(a, b, dims, preferred_element_type=F32)


def low_one_hot(ids, low):
    rows = lax.broadcasted_iota(jnp.int32, (low, ids.shape[1]), 0).astype(BF16)
    return jnp.where(rows == (ids & (low - 1)).astype(BF16), jnp.ones((), BF16), jnp.zeros((), BF16))


def pick_group(stacked, high, groups):
    size = stacked.shape[0] // groups
    picked = stacked[:size]
    for g in range(1, groups):
        picked = jnp.where(high == g, stacked[g * size : (g + 1) * size], picked)
    return picked


def spread_groups(values, high, groups):
    narrow = values.astype(BF16)
    return jnp.concatenate(
        [narrow * jnp.where(high == g, 1.0, 0.0).astype(BF16) for g in range(groups)], axis=0
    )


def eye(size):
    rows = lax.broadcasted_iota(jnp.int32, (size, size), 0)
    return rows == lax.broadcasted_iota(jnp.int32, (size, size), 1)


def forward_kernel(
    span,
    live_ref,
    latent_hbm,
    head_hbm,
    bias_hbm,
    targets_hbm,
    cell_hbm,
    pixel_hbm,
    weight_hbm,
    frame_ref,
    west_ref,
    east_ref,
    latent_ref,
    head_ref,
    cell_ref,
    pixel_ref,
    weight_ref,
    bias_ref,
    targets_ref,
    predicted,
    wide_targets,
    sems,
):
    copies = [
        pltpu.make_async_copy(source, target, sems.at[i])
        for i, (source, target) in enumerate(
            (
                (latent_hbm, latent_ref),
                (head_hbm, head_ref),
                (bias_hbm, bias_ref),
                (cell_hbm, cell_ref),
                (pixel_hbm, pixel_ref),
                (weight_hbm, weight_ref),
                (targets_hbm, targets_ref),
            )
        )
    ]
    for copy in copies:
        copy.start()
    cycles, low_cells, _ = latent_ref.shape
    variables, tile_rows, tile_cols = targets_ref.shape
    frame_width = 2 * tile_cols
    rim = tile_cols // 2
    frame_ref[...] = jnp.zeros_like(frame_ref)
    for copy in copies[:]:
        copy.wait()
    bias = jnp.sum(jnp.where(eye(variables), bias_ref[...], 0.0), axis=1, keepdims=True)
    for c in range(cycles):
        predicted[c * variables : (c + 1) * variables, :] = (
            dot(head_ref[...], latent_ref[c], NT) + bias
        ).astype(BF16)
    rows = lax.broadcasted_iota(jnp.int32, weight_ref.shape, 1)
    weight_ref[...] = jnp.where(rows < live_ref[0, 0], weight_ref[...], 0.0)
    wide_targets[...] = targets_ref[...].astype(F32)
    for t in range(tile_rows):
        rows = slice(t * variables, (t + 1) * variables)
        frame_ref[rows, rim : rim + tile_cols] = -wide_targets[:, t, :]
    for start in range(0, cell_ref.shape[1], span):
        cell = cell_ref[:, pl.ds(start, span)]
        pixel = pixel_ref[:, pl.ds(start, span)]
        weight = weight_ref[:, pl.ds(start, span)]
        gathered = dot(predicted[...], low_one_hot(cell, low_cells), NN)
        share = pick_group(gathered, cell // low_cells, cycles) * weight
        frame_ref[...] += dot(
            spread_groups(share, pixel // frame_width, tile_rows),
            low_one_hot(pixel, frame_width),
            NT,
        )
    west_ref[...] = frame_ref[:, :tile_cols].astype(BF16)
    east_ref[...] = frame_ref[:, tile_cols:].astype(BF16)


def gather_latent_kernel(span, latent_ref, cell_ref, gathered_ref, table):
    cycles, low_cells, width = latent_ref.shape
    for c in range(cycles):
        table[c * width : (c + 1) * width, :] = latent_ref[c].astype(F32).T.astype(BF16)
    for start in range(0, gathered_ref.shape[1], span):
        cell = cell_ref[:, pl.ds(start, span)]
        gathered = dot(table[...], low_one_hot(cell, low_cells), NN)
        gathered_ref[:, pl.ds(start, span)] = pick_group(
            gathered, cell // low_cells, cycles
        ).astype(BF16)


def backward_kernel(
    span,
    tile_rows,
    frame_ref,
    from_west_ref,
    from_east_ref,
    latent_ref,
    cell_ref,
    pixel_ref,
    weight_ref,
    row_latent_ref,
    share_ref,
    totals_ref,
    part_ref,
    misfit,
):
    cycles, low_cells, width = latent_ref.shape
    early = row_latent_ref.shape[1]
    frame_rows, frame_width = frame_ref.shape
    variables = frame_rows // tile_rows
    half = frame_width // 2
    misfit[:, :half] = (frame_ref[:, :half] + from_west_ref[...].astype(F32)).astype(BF16)
    misfit[:, half:] = (frame_ref[:, half:] + from_east_ref[...].astype(F32)).astype(BF16)
    head_part = jnp.zeros((variables, width), F32)
    bias_part = jnp.zeros((variables, 128), F32)
    totals_ref[...] = jnp.zeros_like(totals_ref)
    for start in reversed(range(0, pixel_ref.shape[1], span)):
        pixel = pixel_ref[:, pl.ds(start, span)]
        gathered = dot(misfit[...], low_one_hot(pixel, frame_width), NN)
        share = (
            pick_group(gathered, pixel // frame_width, tile_rows)
            * weight_ref[:, pl.ds(start, span)]
        )
        for lane in range(0, span, 128):
            bias_part += share[:, lane : lane + 128]
        if start < early:
            narrow = share.astype(BF16)
            share_ref[:, pl.ds(start, span)] = narrow
        else:
            cell = cell_ref[:, pl.ds(start, span)]
            totals_ref[...] += dot(
                spread_groups(share, cell // low_cells, cycles), low_one_hot(cell, low_cells), NT
            )
    for c in range(cycles):
        rows = slice(c * variables, (c + 1) * variables)
        head_part += dot(totals_ref[rows, :].astype(BF16), latent_ref[c], NN)
    head_part += dot(share_ref[...], row_latent_ref[...], NT)
    part_ref[...] = jnp.zeros_like(part_ref)
    part_ref[:variables, :] = head_part
    part_ref[variables : variables + 1, :variables] = jnp.sum(
        jnp.where(eye(variables), jnp.sum(bias_part, axis=1, keepdims=True), 0.0),
        axis=0,
        keepdims=True,
    )


def cell_kernel(span, share_ref, cell_ref, late_ref, cell_misfit_ref, totals):
    variables, early = share_ref.shape
    groups, low_cells = totals.shape[0] // variables, totals.shape[1]
    totals[...] = late_ref[...]
    for start in range(0, early, span):
        cell = cell_ref[:, pl.ds(start, span)]
        totals[...] += dot(
            spread_groups(share_ref[:, pl.ds(start, span)], cell // low_cells, groups),
            low_one_hot(cell, low_cells),
            NT,
        )
    cell_misfit_ref[...] = totals[...].astype(BF16)


def latent_kernel(cell_misfit_ref, head_ref, latent_grad_ref):
    variables = head_ref.shape[0]
    for c in range(latent_grad_ref.shape[0]):
        rows = slice(c * variables, (c + 1) * variables)
        wide = cell_misfit_ref[rows, :].astype(F32)
        latent_grad_ref[c] = dot(wide.T.astype(BF16), head_ref[...], NN).astype(BF16)


def finish_kernel(scale, mine_ref, theirs_ref, head_grad_ref, bias_grad_ref):
    variables = head_grad_ref.shape[0]
    head_grad_ref[...] = (mine_ref[:variables, :] + theirs_ref[:variables, :]) * scale
    last = slice(variables, variables + 1)
    bias_grad_ref[...] = (mine_ref[last, :variables] + theirs_ref[last, :variables]) * scale


def sum_rounds(lat, lon):
    rounds = []
    low_first = [1 << k for k in range(lat.bit_length() - 1)]
    while low_first:
        pair, low_first = low_first[:2], low_first[2:]
        rounds.append([(s, 0) for s in pair + [pair[0] ^ pair[-1]] * (len(pair) - 1)])
    cross = min(lat - 1, 1)
    high_first = [1 << k for k in reversed(range(lon.bit_length() - 1))]
    while high_first:
        take = 2 - len(high_first) % 2
        pair, high_first = high_first[:take], high_first[take:]
        rounds.append([(cross, s) for s in pair + [pair[0] ^ pair[-1]] * (take - 1)])
    return rounds


def add_pairs(values):
    while len(values) > 1:
        values = [values[i] + values[i + 1] for i in range(0, len(values), 2)]
    return values[0]


def sum_but_last(value, jobs):
    lat, lon = lax.axis_size("lat"), lax.axis_size("lon")

    def swap(shard, flip):
        pairs = [
            (i * lon + j, (i ^ flip[0]) * lon + (j ^ flip[1])) for i in range(lat) for j in range(lon)
        ]
        return lax.ppermute(shard, ("lat", "lon"), pairs)

    jobs, done = list(jobs), None
    powers = lat & (lat - 1) == 0 and lon & (lon - 1) == 0
    rounds = sum_rounds(lat, lon) if powers else []
    for flips in rounds[:-1]:
        shards = [value] + [swap(value, flip) for flip in flips]
        if jobs:
            done = jobs.pop(0)(done)
            value, done = lax.optimization_barrier((add_pairs(shards), done))
        else:
            value = add_pairs(shards)
    for job in jobs:
        done = job(done)
    if not rounds:
        return lax.psum(value, ("lat", "lon")), jnp.zeros_like(value), done
    last = [value] + [swap(value, flip) for flip in rounds[-1]]
    half = len(last) // 2
    return add_pairs(last[:half]), add_pairs(last[half:]), done


def from_behind(shard, axis, by):
    devices = lax.axis_size(axis)
    return lax.ppermute(shard, axis, [(i, (i + by) % devices) for i in range(devices)])


def per_device(latent, head, bias, targets, margin_cell, margin_pixel, margin_weight, live_count):
    cycles, low_cells, width = latent.shape
    variables, tile_rows, tile_cols = targets.shape
    frame_shape = (tile_rows * variables, 2 * tile_cols)
    half_shape = (tile_rows * variables, tile_cols)
    cell_shape = (cycles * variables, low_cells)
    cell = margin_cell.reshape(1, -1)
    pixel = margin_pixel.reshape(1, -1)
    weight = margin_weight.reshape(1, -1)
    span = math.gcd(1024, cell.shape[1])
    hbm = pl.BlockSpec(memory_space=pltpu.HBM)
    vmem = pl.BlockSpec(memory_space=pltpu.VMEM)
    params = pltpu.CompilerParams(vmem_limit_bytes=24 * 1024 * 1024)
    frame, west, east, latent, head_t, cell, pixel, weight = pl.pallas_call(
        functools.partial(forward_kernel, span),
        out_shape=(
            jax.ShapeDtypeStruct(frame_shape, F32),
            jax.ShapeDtypeStruct(half_shape, BF16),
            jax.ShapeDtypeStruct(half_shape, BF16),
            jax.ShapeDtypeStruct(latent.shape, BF16),
            jax.ShapeDtypeStruct((variables, width), BF16),
            jax.ShapeDtypeStruct(cell.shape, jnp.int32),
            jax.ShapeDtypeStruct(cell.shape, jnp.int32),
            jax.ShapeDtypeStruct(cell.shape, F32),
        ),
        in_specs=[pl.BlockSpec(memory_space=pltpu.SMEM)] + [hbm] * 7,
        out_specs=[vmem] * 8,
        scratch_shapes=[
            pltpu.VMEM((1, variables), F32),
            pltpu.VMEM(targets.shape, BF16),
            pltpu.VMEM(cell_shape, BF16),
            pltpu.VMEM((variables, tile_rows, tile_cols), F32),
            pltpu.SemaphoreType.DMA((7,)),
        ],
        compiler_params=params,
        name="forward",
    )(
        live_count,
        *(
            pltpu.with_memory_space_constraint(array, pltpu.HBM)
            for array in (latent, head.T, bias.reshape(1, -1), targets, cell, pixel, weight)
        ),
    )
    from_west = from_behind(east, "lon", 1)
    from_east = from_behind(west, "lon", -1)
    row_total = cell.shape[1]
    early = row_total * 2 // 3 // span * span
    row_latent = pl.pallas_call(
        functools.partial(gather_latent_kernel, span),
        out_shape=jax.ShapeDtypeStruct((width, early), BF16),
        in_specs=[vmem, vmem],
        out_specs=vmem,
        scratch_shapes=[pltpu.VMEM((cycles * width, low_cells), BF16)],
        compiler_params=params,
        cost_estimate=pl.CostEstimate(
            flops=2 * cycles * width * low_cells * early,
            bytes_accessed=2 * width * early,
            transcendentals=0,
        ),
        name="gather_latent",
    )(latent, cell)
    share, totals, part = pl.pallas_call(
        functools.partial(backward_kernel, span, tile_rows),
        out_shape=(
            jax.ShapeDtypeStruct((variables, early), BF16),
            jax.ShapeDtypeStruct(cell_shape, F32),
            jax.ShapeDtypeStruct((variables + 8, width), F32),
        ),
        in_specs=[vmem] * 8,
        out_specs=(vmem, vmem, vmem),
        scratch_shapes=[pltpu.VMEM(frame_shape, BF16)],
        compiler_params=params,
        name="backward",
    )(frame, from_west, from_east, latent, cell, pixel, weight, row_latent)

    def add_early_cells(_):
        return pl.pallas_call(
            functools.partial(cell_kernel, span),
            out_shape=jax.ShapeDtypeStruct(cell_shape, BF16),
            in_specs=[vmem] * 3,
            out_specs=vmem,
            scratch_shapes=[pltpu.VMEM(cell_shape, F32)],
            compiler_params=params,
            cost_estimate=pl.CostEstimate(
                flops=2 * cycles * variables * low_cells * row_total,
                bytes_accessed=2 * variables * row_total,
                transcendentals=0,
            ),
            name="cells",
        )(share, cell, totals)

    def grad_of_latent(cell_misfit):
        return pl.pallas_call(
            latent_kernel,
            out_shape=jax.ShapeDtypeStruct(latent.shape, BF16),
            in_specs=[vmem, vmem],
            out_specs=vmem,
            compiler_params=params,
            cost_estimate=pl.CostEstimate(
                flops=2 * cycles * low_cells * width * variables,
                bytes_accessed=2 * cycles * low_cells * width,
                transcendentals=0,
            ),
            name="latent_gradient",
        )(cell_misfit, head_t)

    mine, theirs, latent_grad = sum_but_last(part, (add_early_cells, grad_of_latent))
    cell_total = cycles * low_cells * lax.axis_size("lat") * lax.axis_size("lon")
    head_grad, bias_grad = pl.pallas_call(
        functools.partial(finish_kernel, 1.0 / math.sqrt(cell_total)),
        out_shape=(
            jax.ShapeDtypeStruct((variables, width), F32),
            jax.ShapeDtypeStruct((1, variables), F32),
        ),
        in_specs=[vmem, vmem],
        out_specs=(vmem, vmem),
        compiler_params=pltpu.CompilerParams(vmem_limit_bytes=1024 * 1024),
        name="finish",
    )(mine, theirs)
    return latent_grad, head_grad.T, bias_grad.reshape(variables)


def solution(mesh):
    in_specs = (
        P("lat", "lon", None),
        P(),
        P(),
        P(None, "lat", "lon"),
        P("lat", "lon", None),
        P("lat", "lon", None),
        P("lat", "lon", None),
        P("lat", "lon"),
    )
    out_specs = (P("lat", "lon", None), P(), P())
    return jax.shard_map(
        per_device, mesh=mesh, in_specs=in_specs, out_specs=out_specs, check_vma=False
    )
```

```python
import functools
import math

import jax
import jax.numpy as jnp
from jax import lax
from jax.experimental import pallas as pl
from jax.experimental.pallas import tpu as pltpu
from jax.sharding import PartitionSpec as P

BF16 = jnp.bfloat16
F32 = jnp.float32
NN = (((1,), (0,)), ((), ()))
NT = (((1,), (1,)), ((), ()))


def dot(a, b, dims):
    return lax.dot_general(a, b, dims, preferred_element_type=F32)


def low_one_hot(ids, low):
    rows = lax.broadcasted_iota(jnp.int32, (low, ids.shape[1]), 0).astype(BF16)
    return jnp.where(rows == (ids & (low - 1)).astype(BF16), jnp.ones((), BF16), jnp.zeros((), BF16))


def pick_group(stacked, high, groups):
    size = stacked.shape[0] // groups
    picked = stacked[:size]
    for g in range(1, groups):
        picked = jnp.where(high == g, stacked[g * size : (g + 1) * size], picked)
    return picked


def spread_groups(values, high, groups):
    narrow = values.astype(BF16)
    return jnp.concatenate(
        [narrow * jnp.where(high == g, 1.0, 0.0).astype(BF16) for g in range(groups)], axis=0
    )


def eye(size):
    rows = lax.broadcasted_iota(jnp.int32, (size, size), 0)
    return rows == lax.broadcasted_iota(jnp.int32, (size, size), 1)


def forward_kernel(
    span,
    live_ref,
    latent_hbm,
    head_given,
    bias_hbm,
    targets_hbm,
    cell_hbm,
    pixel_hbm,
    weight_hbm,
    frame_ref,
    west_ref,
    east_ref,
    latent_ref,
    head_ref,
    cell_ref,
    pixel_ref,
    weight_ref,
    bias_ref,
    targets_ref,
    predicted,
    wide_targets,
    placed,
    columns,
    sems,
):
    copies = [
        pltpu.make_async_copy(source, target, sems.at[i])
        for i, (source, target) in enumerate(
            (
                (latent_hbm, latent_ref),
                (bias_hbm, bias_ref),
                (cell_hbm, cell_ref),
                (pixel_hbm, pixel_ref),
                (weight_hbm, weight_ref),
                (targets_hbm, targets_ref),
            )
        )
    ]
    for copy in copies:
        copy.start()
    cycles, low_cells, _ = latent_ref.shape
    variables, tile_rows, tile_cols = targets_ref.shape
    frame_width = 2 * tile_cols
    rim = tile_cols // 2
    frame_ref[...] = jnp.zeros_like(frame_ref)
    for copy in copies:
        copy.wait()
    bias = jnp.sum(jnp.where(eye(variables), bias_ref[...], 0.0), axis=1, keepdims=True)
    head_ref[...] = head_given[...]
    for c in range(cycles):
        predicted[c * variables : (c + 1) * variables, :] = (
            dot(head_ref[...], latent_ref[c], NT) + bias
        ).astype(BF16)
    rows = lax.broadcasted_iota(jnp.int32, weight_ref.shape, 1)
    weight_ref[...] = jnp.where(rows < live_ref[0, 0], weight_ref[...], 0.0)
    wide_targets[...] = targets_ref[...].astype(F32)
    for t in range(tile_rows):
        rows = slice(t * variables, (t + 1) * variables)
        frame_ref[rows, rim : rim + tile_cols] = -wide_targets[:, t, :]
    for start in range(0, cell_ref.shape[1], span):
        cell = cell_ref[:, pl.ds(start, span)]
        pixel = pixel_ref[:, pl.ds(start, span)]
        weight = weight_ref[:, pl.ds(start, span)]
        gathered = dot(predicted[...], low_one_hot(cell, low_cells), NN)
        share = pick_group(gathered, cell // low_cells, cycles) * weight
        placed[:, pl.ds(start, span)] = spread_groups(share, pixel // frame_width, tile_rows)
        columns[:, pl.ds(start, span)] = low_one_hot(pixel, frame_width)
    frame_ref[...] += dot(placed[...], columns[...], NT)
    west_ref[...] = frame_ref[:, :tile_cols].astype(BF16)
    east_ref[...] = frame_ref[:, tile_cols:].astype(BF16)


def gather_latent_kernel(span, latent_ref, cell_ref, gathered_ref, table):
    cycles, low_cells, width = latent_ref.shape
    for c in range(cycles):
        table[c * width : (c + 1) * width, :] = latent_ref[c].astype(F32).T.astype(BF16)
    for start in range(0, gathered_ref.shape[1], span):
        cell = cell_ref[:, pl.ds(start, span)]
        gathered = dot(table[...], low_one_hot(cell, low_cells), NN)
        gathered_ref[:, pl.ds(start, span)] = pick_group(
            gathered, cell // low_cells, cycles
        ).astype(BF16)


def backward_kernel(
    span,
    tile_rows,
    frame_ref,
    from_west_ref,
    from_east_ref,
    latent_ref,
    cell_ref,
    pixel_ref,
    weight_ref,
    row_latent_ref,
    share_ref,
    totals_ref,
    part_ref,
    misfit,
):
    cycles, low_cells, width = latent_ref.shape
    early = row_latent_ref.shape[1]
    frame_rows, frame_width = frame_ref.shape
    variables = frame_rows // tile_rows
    half = frame_width // 2
    misfit[:, :half] = (frame_ref[:, :half] + from_west_ref[...].astype(F32)).astype(BF16)
    misfit[:, half:] = (frame_ref[:, half:] + from_east_ref[...].astype(F32)).astype(BF16)
    head_part = jnp.zeros((variables, width), F32)
    bias_part = jnp.zeros((variables, 128), F32)
    totals_ref[...] = jnp.zeros_like(totals_ref)
    for start in reversed(range(0, pixel_ref.shape[1], span)):
        pixel = pixel_ref[:, pl.ds(start, span)]
        gathered = dot(misfit[...], low_one_hot(pixel, frame_width), NN)
        share = (
            pick_group(gathered, pixel // frame_width, tile_rows)
            * weight_ref[:, pl.ds(start, span)]
        )
        for lane in range(0, span, 128):
            bias_part += share[:, lane : lane + 128]
        if start < early:
            narrow = share.astype(BF16)
            share_ref[:, pl.ds(start, span)] = narrow
        else:
            cell = cell_ref[:, pl.ds(start, span)]
            totals_ref[...] += dot(
                spread_groups(share, cell // low_cells, cycles), low_one_hot(cell, low_cells), NT
            )
    for c in range(cycles):
        rows = slice(c * variables, (c + 1) * variables)
        head_part += dot(totals_ref[rows, :].astype(BF16), latent_ref[c], NN)
    head_part += dot(share_ref[...], row_latent_ref[...], NT)
    part_ref[...] = jnp.zeros_like(part_ref)
    part_ref[:variables, :] = head_part
    part_ref[variables : variables + 1, :variables] = jnp.sum(
        jnp.where(eye(variables), jnp.sum(bias_part, axis=1, keepdims=True), 0.0),
        axis=0,
        keepdims=True,
    )


def cell_kernel(span, share_ref, cell_ref, late_ref, cell_misfit_ref, totals):
    variables, early = share_ref.shape
    groups, low_cells = totals.shape[0] // variables, totals.shape[1]
    totals[...] = late_ref[...]
    for start in range(0, early, span):
        cell = cell_ref[:, pl.ds(start, span)]
        totals[...] += dot(
            spread_groups(share_ref[:, pl.ds(start, span)], cell // low_cells, groups),
            low_one_hot(cell, low_cells),
            NT,
        )
    cell_misfit_ref[...] = totals[...].astype(BF16)


def latent_kernel(cell_misfit_ref, head_ref, latent_grad_ref):
    variables = head_ref.shape[0]
    for c in range(latent_grad_ref.shape[0]):
        rows = slice(c * variables, (c + 1) * variables)
        wide = cell_misfit_ref[rows, :].astype(F32)
        latent_grad_ref[c] = dot(wide.T.astype(BF16), head_ref[...], NN).astype(BF16)


def finish_kernel(scale, mine_ref, theirs_ref, head_grad_ref, bias_grad_ref):
    variables = head_grad_ref.shape[0]
    head_grad_ref[...] = (mine_ref[:variables, :] + theirs_ref[:variables, :]) * scale
    last = slice(variables, variables + 1)
    bias_grad_ref[...] = (mine_ref[last, :variables] + theirs_ref[last, :variables]) * scale


def sum_rounds(lat, lon):
    rounds = []
    low_first = [1 << k for k in range(lat.bit_length() - 1)]
    while low_first:
        pair, low_first = low_first[:2], low_first[2:]
        rounds.append([(s, 0) for s in pair + [pair[0] ^ pair[-1]] * (len(pair) - 1)])
    cross = min(lat - 1, 1)
    high_first = [1 << k for k in reversed(range(lon.bit_length() - 1))]
    while high_first:
        take = 2 - len(high_first) % 2
        pair, high_first = high_first[:take], high_first[take:]
        rounds.append([(cross, s) for s in pair + [pair[0] ^ pair[-1]] * (take - 1)])
    return rounds


def add_pairs(values):
    while len(values) > 1:
        values = [values[i] + values[i + 1] for i in range(0, len(values), 2)]
    return values[0]


def sum_but_last(value, jobs):
    lat, lon = lax.axis_size("lat"), lax.axis_size("lon")

    def swap(shard, flip):
        pairs = [
            (i * lon + j, (i ^ flip[0]) * lon + (j ^ flip[1])) for i in range(lat) for j in range(lon)
        ]
        return lax.ppermute(shard, ("lat", "lon"), pairs)

    jobs, done = list(jobs), None
    powers = lat & (lat - 1) == 0 and lon & (lon - 1) == 0
    rounds = sum_rounds(lat, lon) if powers else []
    for flips in rounds[:-1]:
        shards = [value] + [swap(value, flip) for flip in flips]
        if jobs:
            done = jobs.pop(0)(done)
            value, done = lax.optimization_barrier((add_pairs(shards), done))
        else:
            value = add_pairs(shards)
    for job in jobs:
        done = job(done)
    if not rounds:
        return lax.psum(value, ("lat", "lon")), jnp.zeros_like(value), done
    last = [value] + [swap(value, flip) for flip in rounds[-1]]
    half = len(last) // 2
    return add_pairs(last[:half]), add_pairs(last[half:]), done


def from_behind(shard, axis, by):
    devices = lax.axis_size(axis)
    return lax.ppermute(shard, axis, [(i, (i + by) % devices) for i in range(devices)])


def per_device(latent, head, bias, targets, margin_cell, margin_pixel, margin_weight, live_count):
    cycles, low_cells, width = latent.shape
    variables, tile_rows, tile_cols = targets.shape
    frame_shape = (tile_rows * variables, 2 * tile_cols)
    half_shape = (tile_rows * variables, tile_cols)
    cell_shape = (cycles * variables, low_cells)
    cell = margin_cell.reshape(1, -1)
    pixel = margin_pixel.reshape(1, -1)
    weight = margin_weight.reshape(1, -1)
    span = math.gcd(1024, cell.shape[1])
    hbm = pl.BlockSpec(memory_space=pltpu.HBM)
    vmem = pl.BlockSpec(memory_space=pltpu.VMEM)
    params = pltpu.CompilerParams(vmem_limit_bytes=24 * 1024 * 1024)
    frame, west, east, latent, head_t, cell, pixel, weight = pl.pallas_call(
        functools.partial(forward_kernel, span),
        out_shape=(
            jax.ShapeDtypeStruct(frame_shape, F32),
            jax.ShapeDtypeStruct(half_shape, BF16),
            jax.ShapeDtypeStruct(half_shape, BF16),
            jax.ShapeDtypeStruct(latent.shape, BF16),
            jax.ShapeDtypeStruct((variables, width), BF16),
            jax.ShapeDtypeStruct(cell.shape, jnp.int32),
            jax.ShapeDtypeStruct(cell.shape, jnp.int32),
            jax.ShapeDtypeStruct(cell.shape, F32),
        ),
        in_specs=[pl.BlockSpec(memory_space=pltpu.SMEM), hbm, vmem, hbm, hbm, hbm, hbm, hbm],
        out_specs=[vmem] * 8,
        scratch_shapes=[
            pltpu.VMEM((1, variables), F32),
            pltpu.VMEM(targets.shape, BF16),
            pltpu.VMEM(cell_shape, BF16),
            pltpu.VMEM((variables, tile_rows, tile_cols), F32),
            pltpu.VMEM((frame_shape[0], cell.shape[1]), BF16),
            pltpu.VMEM((frame_shape[1], cell.shape[1]), BF16),
            pltpu.SemaphoreType.DMA((6,)),
        ],
        compiler_params=params,
        name="forward",
    )(
        live_count,
        pltpu.with_memory_space_constraint(latent, pltpu.HBM),
        head.T,
        pltpu.with_memory_space_constraint(bias.reshape(1, -1), pltpu.HBM),
        pltpu.with_memory_space_constraint(targets, pltpu.HBM),
        pltpu.with_memory_space_constraint(cell, pltpu.HBM),
        pltpu.with_memory_space_constraint(pixel, pltpu.HBM),
        pltpu.with_memory_space_constraint(weight, pltpu.HBM),
    )
    from_west = from_behind(east, "lon", 1)
    from_east = from_behind(west, "lon", -1)
    row_total = cell.shape[1]
    early = row_total * 2 // 3 // span * span
    row_latent = pl.pallas_call(
        functools.partial(gather_latent_kernel, span),
        out_shape=jax.ShapeDtypeStruct((width, early), BF16),
        in_specs=[vmem, vmem],
        out_specs=vmem,
        scratch_shapes=[pltpu.VMEM((cycles * width, low_cells), BF16)],
        compiler_params=params,
        cost_estimate=pl.CostEstimate(
            flops=2 * cycles * width * low_cells * early,
            bytes_accessed=2 * width * early,
            transcendentals=0,
        ),
        name="gather_latent",
    )(latent, cell)
    share, totals, part = pl.pallas_call(
        functools.partial(backward_kernel, span, tile_rows),
        out_shape=(
            jax.ShapeDtypeStruct((variables, early), BF16),
            jax.ShapeDtypeStruct(cell_shape, F32),
            jax.ShapeDtypeStruct((variables + 8, width), F32),
        ),
        in_specs=[vmem] * 8,
        out_specs=(vmem, vmem, vmem),
        scratch_shapes=[pltpu.VMEM(frame_shape, BF16)],
        compiler_params=params,
        name="backward",
    )(frame, from_west, from_east, latent, cell, pixel, weight, row_latent)

    def add_early_cells(_):
        return pl.pallas_call(
            functools.partial(cell_kernel, span),
            out_shape=jax.ShapeDtypeStruct(cell_shape, BF16),
            in_specs=[vmem] * 3,
            out_specs=vmem,
            scratch_shapes=[pltpu.VMEM(cell_shape, F32)],
            compiler_params=params,
            cost_estimate=pl.CostEstimate(
                flops=2 * cycles * variables * low_cells * row_total,
                bytes_accessed=2 * variables * row_total,
                transcendentals=0,
            ),
            name="cells",
        )(share, cell, totals)

    def grad_of_latent(cell_misfit):
        return pl.pallas_call(
            latent_kernel,
            out_shape=jax.ShapeDtypeStruct(latent.shape, BF16),
            in_specs=[vmem, vmem],
            out_specs=vmem,
            compiler_params=params,
            cost_estimate=pl.CostEstimate(
                flops=2 * cycles * low_cells * width * variables,
                bytes_accessed=2 * cycles * low_cells * width,
                transcendentals=0,
            ),
            name="latent_gradient",
        )(cell_misfit, head_t)

    mine, theirs, latent_grad = sum_but_last(part, (add_early_cells, grad_of_latent))
    cell_total = cycles * low_cells * lax.axis_size("lat") * lax.axis_size("lon")
    head_grad, bias_grad = pl.pallas_call(
        functools.partial(finish_kernel, 1.0 / math.sqrt(cell_total)),
        out_shape=(
            jax.ShapeDtypeStruct((variables, width), F32),
            jax.ShapeDtypeStruct((1, variables), F32),
        ),
        in_specs=[vmem, vmem],
        out_specs=(vmem, vmem),
        compiler_params=pltpu.CompilerParams(vmem_limit_bytes=1024 * 1024),
        name="finish",
    )(mine, theirs)
    return latent_grad, head_grad.T, bias_grad.reshape(variables)


def solution(mesh):
    in_specs = (
        P("lat", "lon", None),
        P(),
        P(),
        P(None, "lat", "lon"),
        P("lat", "lon", None),
        P("lat", "lon", None),
        P("lat", "lon", None),
        P("lat", "lon"),
    )
    out_specs = (P("lat", "lon", None), P(), P())
    return jax.shard_map(
        per_device, mesh=mesh, in_specs=in_specs, out_specs=out_specs, check_vma=False
    )
```

```python
import functools
import math

import jax
import jax.numpy as jnp
from jax import lax
from jax.experimental import pallas as pl
from jax.experimental.pallas import tpu as pltpu
from jax.sharding import PartitionSpec as P

BF16 = jnp.bfloat16
F32 = jnp.float32
NN = (((1,), (0,)), ((), ()))
NT = (((1,), (1,)), ((), ()))


def dot(a, b, dims):
    return lax.dot_general(a, b, dims, preferred_element_type=F32)


def low_one_hot(ids, low):
    rows = lax.broadcasted_iota(jnp.int32, (low, ids.shape[1]), 0).astype(BF16)
    return jnp.where(rows == (ids & (low - 1)).astype(BF16), jnp.ones((), BF16), jnp.zeros((), BF16))


def pick_group(stacked, high, groups):
    size = stacked.shape[0] // groups
    picked = stacked[:size]
    for g in range(1, groups):
        picked = jnp.where(high == g, stacked[g * size : (g + 1) * size], picked)
    return picked


def spread_groups(values, high, groups):
    narrow = values.astype(BF16)
    return jnp.concatenate(
        [narrow * jnp.where(high == g, 1.0, 0.0).astype(BF16) for g in range(groups)], axis=0
    )


def eye(size):
    rows = lax.broadcasted_iota(jnp.int32, (size, size), 0)
    return rows == lax.broadcasted_iota(jnp.int32, (size, size), 1)


def forward_kernel(
    span,
    live_ref,
    latent_hbm,
    head_given,
    bias_hbm,
    targets_hbm,
    cell_hbm,
    pixel_hbm,
    weight_hbm,
    frame_ref,
    west_ref,
    east_ref,
    latent_ref,
    head_ref,
    cell_ref,
    pixel_ref,
    weight_ref,
    bias_ref,
    targets_ref,
    predicted,
    wide_targets,
    placed,
    columns,
    sems,
):
    copies = [
        pltpu.make_async_copy(source, target, sems.at[i])
        for i, (source, target) in enumerate(
            (
                (latent_hbm, latent_ref),
                (bias_hbm, bias_ref),
                (cell_hbm, cell_ref),
                (pixel_hbm, pixel_ref),
                (weight_hbm, weight_ref),
                (targets_hbm, targets_ref),
            )
        )
    ]
    for copy in copies:
        copy.start()
    cycles, low_cells, _ = latent_ref.shape
    variables, tile_rows, tile_cols = targets_ref.shape
    frame_width = 2 * tile_cols
    rim = tile_cols // 2
    frame_ref[...] = jnp.zeros_like(frame_ref)
    for copy in copies:
        copy.wait()
    bias = jnp.sum(jnp.where(eye(variables), bias_ref[...], 0.0), axis=1, keepdims=True)
    head_ref[...] = head_given[...]
    for c in range(cycles):
        predicted[c * variables : (c + 1) * variables, :] = (
            dot(head_ref[...], latent_ref[c], NT) + bias
        ).astype(BF16)
    rows = lax.broadcasted_iota(jnp.int32, weight_ref.shape, 1)
    weight_ref[...] = jnp.where(rows < live_ref[0, 0], weight_ref[...], 0.0)
    wide_targets[...] = targets_ref[...].astype(F32)
    for t in range(tile_rows):
        rows = slice(t * variables, (t + 1) * variables)
        frame_ref[rows, rim : rim + tile_cols] = -wide_targets[:, t, :]
    for start in range(0, cell_ref.shape[1], span):
        cell = cell_ref[:, pl.ds(start, span)]
        pixel = pixel_ref[:, pl.ds(start, span)]
        weight = weight_ref[:, pl.ds(start, span)]
        gathered = dot(predicted[...], low_one_hot(cell, low_cells), NN)
        share = pick_group(gathered, cell // low_cells, cycles) * weight
        placed[:, pl.ds(start, span)] = spread_groups(share, pixel // frame_width, tile_rows)
        columns[:, pl.ds(start, span)] = low_one_hot(pixel, frame_width)
    frame_ref[...] += dot(placed[...], columns[...], NT)
    west_ref[...] = frame_ref[:, :tile_cols].astype(BF16)
    east_ref[...] = frame_ref[:, tile_cols:].astype(BF16)


def gather_latent_kernel(span, latent_ref, cell_ref, gathered_ref, table):
    cycles, low_cells, width = latent_ref.shape
    for c in range(cycles):
        table[c * width : (c + 1) * width, :] = latent_ref[c].astype(F32).T.astype(BF16)
    for start in range(0, gathered_ref.shape[1], span):
        cell = cell_ref[:, pl.ds(start, span)]
        gathered = dot(table[...], low_one_hot(cell, low_cells), NN)
        gathered_ref[:, pl.ds(start, span)] = pick_group(
            gathered, cell // low_cells, cycles
        ).astype(BF16)


def backward_kernel(
    span,
    tile_rows,
    frame_ref,
    from_west_ref,
    from_east_ref,
    latent_ref,
    cell_ref,
    pixel_ref,
    weight_ref,
    row_latent_ref,
    share_ref,
    totals_ref,
    part_ref,
    misfit,
):
    cycles, low_cells, width = latent_ref.shape
    early = row_latent_ref.shape[1]
    frame_rows, frame_width = frame_ref.shape
    variables = frame_rows // tile_rows
    half = frame_width // 2
    misfit[:, :half] = (frame_ref[:, :half] + from_west_ref[...].astype(F32)).astype(BF16)
    misfit[:, half:] = (frame_ref[:, half:] + from_east_ref[...].astype(F32)).astype(BF16)
    head_part = jnp.zeros((variables, width), F32)
    bias_part = jnp.zeros((variables, 128), F32)
    totals_ref[...] = jnp.zeros_like(totals_ref)
    for start in reversed(range(0, pixel_ref.shape[1], span)):
        pixel = pixel_ref[:, pl.ds(start, span)]
        gathered = dot(misfit[...], low_one_hot(pixel, frame_width), NN)
        share = (
            pick_group(gathered, pixel // frame_width, tile_rows)
            * weight_ref[:, pl.ds(start, span)]
        )
        for lane in range(0, span, 128):
            bias_part += share[:, lane : lane + 128]
        if start < early:
            narrow = share.astype(BF16)
            share_ref[:, pl.ds(start, span)] = narrow
        else:
            cell = cell_ref[:, pl.ds(start, span)]
            totals_ref[...] += dot(
                spread_groups(share, cell // low_cells, cycles), low_one_hot(cell, low_cells), NT
            )
    for c in range(cycles):
        rows = slice(c * variables, (c + 1) * variables)
        head_part += dot(totals_ref[rows, :].astype(BF16), latent_ref[c], NN)
    head_part += dot(share_ref[...], row_latent_ref[...], NT)
    part_ref[...] = jnp.zeros_like(part_ref)
    part_ref[:variables, :] = head_part
    part_ref[variables : variables + 1, :variables] = jnp.sum(
        jnp.where(eye(variables), jnp.sum(bias_part, axis=1, keepdims=True), 0.0),
        axis=0,
        keepdims=True,
    )


def cell_kernel(span, share_ref, cell_ref, late_ref, cell_misfit_ref, totals):
    variables, early = share_ref.shape
    groups, low_cells = totals.shape[0] // variables, totals.shape[1]
    totals[...] = late_ref[...]
    for start in range(0, early, span):
        cell = cell_ref[:, pl.ds(start, span)]
        totals[...] += dot(
            spread_groups(share_ref[:, pl.ds(start, span)], cell // low_cells, groups),
            low_one_hot(cell, low_cells),
            NT,
        )
    cell_misfit_ref[...] = totals[...].astype(BF16)


def latent_kernel(cell_misfit_ref, head_ref, latent_grad_ref):
    variables = head_ref.shape[0]
    for c in range(latent_grad_ref.shape[0]):
        rows = slice(c * variables, (c + 1) * variables)
        wide = cell_misfit_ref[rows, :].astype(F32)
        latent_grad_ref[c] = dot(wide.T.astype(BF16), head_ref[...], NN).astype(BF16)


def finish_kernel(scale, mine_ref, theirs_ref, head_grad_ref, bias_grad_ref):
    variables = head_grad_ref.shape[0]
    head_grad_ref[...] = (mine_ref[:variables, :] + theirs_ref[:variables, :]) * scale
    last = slice(variables, variables + 1)
    bias_grad_ref[...] = (mine_ref[last, :variables] + theirs_ref[last, :variables]) * scale


def sum_rounds(lat, lon):
    rounds = []
    low_first = [1 << k for k in range(lat.bit_length() - 1)]
    while low_first:
        pair, low_first = low_first[:2], low_first[2:]
        flips = pair + [pair[0] ^ pair[-1]] * (len(pair) - 1)
        rounds.append([(s, 0) for s in flips[1:] + flips[:1]])
    cross = min(lat - 1, 1)
    high_first = [1 << k for k in reversed(range(lon.bit_length() - 1))]
    while high_first:
        take = 2 - len(high_first) % 2
        pair, high_first = high_first[:take], high_first[take:]
        rounds.append([(cross, s) for s in [pair[0] ^ pair[-1]] * (take - 1) + pair])
    return rounds


def add_pairs(values):
    while len(values) > 1:
        values = [values[i] + values[i + 1] for i in range(0, len(values), 2)]
    return values[0]


def sum_but_last(value, jobs):
    lat, lon = lax.axis_size("lat"), lax.axis_size("lon")

    def swap(shard, flip):
        pairs = [
            (i * lon + j, (i ^ flip[0]) * lon + (j ^ flip[1])) for i in range(lat) for j in range(lon)
        ]
        return lax.ppermute(shard, ("lat", "lon"), pairs).astype(F32)

    jobs, done = list(jobs), None
    powers = lat & (lat - 1) == 0 and lon & (lon - 1) == 0
    rounds = sum_rounds(lat, lon) if powers else []
    for flips in rounds[:-1]:
        narrow = value.astype(BF16)
        shards = [narrow.astype(F32)] + [swap(narrow, flip) for flip in flips]
        if jobs:
            done = jobs.pop(0)(done)
            value, done = lax.optimization_barrier((add_pairs(shards), done))
        else:
            value = add_pairs(shards)
    for job in jobs:
        done = job(done)
    if not rounds:
        return lax.psum(value, ("lat", "lon")), jnp.zeros_like(value), done
    narrow = value.astype(BF16)
    last = [narrow.astype(F32)] + [swap(narrow, flip) for flip in rounds[-1]]
    half = len(last) // 2
    return add_pairs(last[:half]), add_pairs(last[half:]), done


def from_behind(shard, axis, by):
    devices = lax.axis_size(axis)
    return lax.ppermute(shard, axis, [(i, (i + by) % devices) for i in range(devices)])


def per_device(latent, head, bias, targets, margin_cell, margin_pixel, margin_weight, live_count):
    cycles, low_cells, width = latent.shape
    variables, tile_rows, tile_cols = targets.shape
    frame_shape = (tile_rows * variables, 2 * tile_cols)
    half_shape = (tile_rows * variables, tile_cols)
    cell_shape = (cycles * variables, low_cells)
    cell = margin_cell.reshape(1, -1)
    pixel = margin_pixel.reshape(1, -1)
    weight = margin_weight.reshape(1, -1)
    span = math.gcd(1024, cell.shape[1])
    hbm = pl.BlockSpec(memory_space=pltpu.HBM)
    vmem = pl.BlockSpec(memory_space=pltpu.VMEM)
    params = pltpu.CompilerParams(vmem_limit_bytes=24 * 1024 * 1024)
    frame, west, east, latent, head_t, cell, pixel, weight = pl.pallas_call(
        functools.partial(forward_kernel, span),
        out_shape=(
            jax.ShapeDtypeStruct(frame_shape, F32),
            jax.ShapeDtypeStruct(half_shape, BF16),
            jax.ShapeDtypeStruct(half_shape, BF16),
            jax.ShapeDtypeStruct(latent.shape, BF16),
            jax.ShapeDtypeStruct((variables, width), BF16),
            jax.ShapeDtypeStruct(cell.shape, jnp.int32),
            jax.ShapeDtypeStruct(cell.shape, jnp.int32),
            jax.ShapeDtypeStruct(cell.shape, F32),
        ),
        in_specs=[pl.BlockSpec(memory_space=pltpu.SMEM), hbm, vmem, hbm, hbm, hbm, hbm, hbm],
        out_specs=[vmem] * 8,
        scratch_shapes=[
            pltpu.VMEM((1, variables), F32),
            pltpu.VMEM(targets.shape, BF16),
            pltpu.VMEM(cell_shape, BF16),
            pltpu.VMEM((variables, tile_rows, tile_cols), F32),
            pltpu.VMEM((frame_shape[0], cell.shape[1]), BF16),
            pltpu.VMEM((frame_shape[1], cell.shape[1]), BF16),
            pltpu.SemaphoreType.DMA((6,)),
        ],
        compiler_params=params,
        name="forward",
    )(
        live_count,
        pltpu.with_memory_space_constraint(latent, pltpu.HBM),
        head.T,
        pltpu.with_memory_space_constraint(bias.reshape(1, -1), pltpu.HBM),
        pltpu.with_memory_space_constraint(targets, pltpu.HBM),
        pltpu.with_memory_space_constraint(cell, pltpu.HBM),
        pltpu.with_memory_space_constraint(pixel, pltpu.HBM),
        pltpu.with_memory_space_constraint(weight, pltpu.HBM),
    )
    from_west = from_behind(east, "lon", 1)
    from_east = from_behind(west, "lon", -1)
    row_total = cell.shape[1]
    early = row_total * 2 // 3 // span * span
    row_latent = pl.pallas_call(
        functools.partial(gather_latent_kernel, span),
        out_shape=jax.ShapeDtypeStruct((width, early), BF16),
        in_specs=[vmem, vmem],
        out_specs=vmem,
        scratch_shapes=[pltpu.VMEM((cycles * width, low_cells), BF16)],
        compiler_params=params,
        cost_estimate=pl.CostEstimate(
            flops=2 * cycles * width * low_cells * early,
            bytes_accessed=2 * width * early,
            transcendentals=0,
        ),
        name="gather_latent",
    )(latent, cell)
    share, totals, part = pl.pallas_call(
        functools.partial(backward_kernel, span, tile_rows),
        out_shape=(
            jax.ShapeDtypeStruct((variables, early), BF16),
            jax.ShapeDtypeStruct(cell_shape, F32),
            jax.ShapeDtypeStruct((variables + 8, width), F32),
        ),
        in_specs=[vmem] * 8,
        out_specs=(vmem, vmem, vmem),
        scratch_shapes=[pltpu.VMEM(frame_shape, BF16)],
        compiler_params=params,
        name="backward",
    )(frame, from_west, from_east, latent, cell, pixel, weight, row_latent)

    def add_early_cells(_):
        return pl.pallas_call(
            functools.partial(cell_kernel, span),
            out_shape=jax.ShapeDtypeStruct(cell_shape, BF16),
            in_specs=[vmem] * 3,
            out_specs=vmem,
            scratch_shapes=[pltpu.VMEM(cell_shape, F32)],
            compiler_params=params,
            cost_estimate=pl.CostEstimate(
                flops=2 * cycles * variables * low_cells * row_total,
                bytes_accessed=2 * variables * row_total,
                transcendentals=0,
            ),
            name="cells",
        )(share, cell, totals)

    def grad_of_latent(cell_misfit):
        return pl.pallas_call(
            latent_kernel,
            out_shape=jax.ShapeDtypeStruct(latent.shape, BF16),
            in_specs=[vmem, vmem],
            out_specs=vmem,
            compiler_params=params,
            cost_estimate=pl.CostEstimate(
                flops=2 * cycles * low_cells * width * variables,
                bytes_accessed=2 * cycles * low_cells * width,
                transcendentals=0,
            ),
            name="latent_gradient",
        )(cell_misfit, head_t)

    mine, theirs, latent_grad = sum_but_last(part, (add_early_cells, grad_of_latent))
    cell_total = cycles * low_cells * lax.axis_size("lat") * lax.axis_size("lon")
    head_grad, bias_grad = pl.pallas_call(
        functools.partial(finish_kernel, 1.0 / math.sqrt(cell_total)),
        out_shape=(
            jax.ShapeDtypeStruct((variables, width), F32),
            jax.ShapeDtypeStruct((1, variables), F32),
        ),
        in_specs=[vmem, vmem],
        out_specs=(vmem, vmem),
        compiler_params=pltpu.CompilerParams(vmem_limit_bytes=1024 * 1024),
        name="finish",
    )(mine, theirs)
    return latent_grad, head_grad.T, bias_grad.reshape(variables)


def solution(mesh):
    in_specs = (
        P("lat", "lon", None),
        P(),
        P(),
        P(None, "lat", "lon"),
        P("lat", "lon", None),
        P("lat", "lon", None),
        P("lat", "lon", None),
        P("lat", "lon"),
    )
    out_specs = (P("lat", "lon", None), P(), P())
    return jax.shard_map(
        per_device, mesh=mesh, in_specs=in_specs, out_specs=out_specs, check_vma=False
    )
```

```python
import functools
import math

import jax
import jax.numpy as jnp
from jax import lax
from jax.experimental import pallas as pl
from jax.experimental.pallas import tpu as pltpu
from jax.sharding import PartitionSpec as P

BF16 = jnp.bfloat16
F32 = jnp.float32
NN = (((1,), (0,)), ((), ()))
NT = (((1,), (1,)), ((), ()))


def dot(a, b, dims):
    return lax.dot_general(a, b, dims, preferred_element_type=F32)


def low_one_hot(ids, low):
    rows = lax.broadcasted_iota(jnp.int32, (low, ids.shape[1]), 0).astype(BF16)
    return jnp.where(rows == (ids & (low - 1)).astype(BF16), jnp.ones((), BF16), jnp.zeros((), BF16))


def pick_group(stacked, high, groups):
    size = stacked.shape[0] // groups
    picked = stacked[:size]
    for g in range(1, groups):
        picked = jnp.where(high == g, stacked[g * size : (g + 1) * size], picked)
    return picked


def spread_groups(values, high, groups):
    narrow = values.astype(BF16)
    return jnp.concatenate(
        [narrow * jnp.where(high == g, 1.0, 0.0).astype(BF16) for g in range(groups)], axis=0
    )


def eye(size):
    rows = lax.broadcasted_iota(jnp.int32, (size, size), 0)
    return rows == lax.broadcasted_iota(jnp.int32, (size, size), 1)


def forward_kernel(
    span,
    live_ref,
    latent_hbm,
    head_given,
    bias_hbm,
    targets_hbm,
    cell_hbm,
    pixel_hbm,
    weight_hbm,
    frame_ref,
    west_ref,
    east_ref,
    latent_ref,
    head_ref,
    cell_ref,
    pixel_ref,
    weight_ref,
    bias_ref,
    targets_ref,
    predicted,
    wide_targets,
    placed,
    columns,
    sems,
):
    copies = [
        pltpu.make_async_copy(source, target, sems.at[i])
        for i, (source, target) in enumerate(
            (
                (latent_hbm, latent_ref),
                (bias_hbm, bias_ref),
                (cell_hbm, cell_ref),
                (pixel_hbm, pixel_ref),
                (weight_hbm, weight_ref),
                (targets_hbm, targets_ref),
            )
        )
    ]
    for copy in copies:
        copy.start()
    cycles, low_cells, _ = latent_ref.shape
    variables, tile_rows, tile_cols = targets_ref.shape
    frame_width = 2 * tile_cols
    rim = tile_cols // 2
    frame_ref[...] = jnp.zeros_like(frame_ref)
    for copy in copies:
        copy.wait()
    bias = jnp.sum(jnp.where(eye(variables), bias_ref[...], 0.0), axis=1, keepdims=True)
    head_ref[...] = head_given[...]
    for c in range(cycles):
        predicted[c * variables : (c + 1) * variables, :] = (
            dot(head_ref[...], latent_ref[c], NT) + bias
        ).astype(BF16)
    rows = lax.broadcasted_iota(jnp.int32, weight_ref.shape, 1)
    weight_ref[...] = jnp.where(rows < live_ref[0, 0], weight_ref[...], 0.0)
    wide_targets[...] = targets_ref[...].astype(F32)
    for t in range(tile_rows):
        rows = slice(t * variables, (t + 1) * variables)
        frame_ref[rows, rim : rim + tile_cols] = -wide_targets[:, t, :]
    for start in range(0, cell_ref.shape[1], span):
        cell = cell_ref[:, pl.ds(start, span)]
        pixel = pixel_ref[:, pl.ds(start, span)]
        weight = weight_ref[:, pl.ds(start, span)]
        gathered = dot(predicted[...], low_one_hot(cell, low_cells), NN)
        share = pick_group(gathered, cell // low_cells, cycles) * weight
        placed[:, pl.ds(start, span)] = spread_groups(share, pixel // frame_width, tile_rows)
        columns[:, pl.ds(start, span)] = low_one_hot(pixel, frame_width)
    frame_ref[...] += dot(placed[...], columns[...], NT)
    west_ref[...] = frame_ref[:, :tile_cols].astype(BF16)
    east_ref[...] = frame_ref[:, tile_cols:].astype(BF16)


def gather_latent_kernel(span, latent_ref, cell_ref, gathered_ref, table):
    cycles, low_cells, width = latent_ref.shape
    for c in range(cycles):
        table[c * width : (c + 1) * width, :] = latent_ref[c].astype(F32).T.astype(BF16)
    for start in range(0, gathered_ref.shape[1], span):
        cell = cell_ref[:, pl.ds(start, span)]
        gathered = dot(table[...], low_one_hot(cell, low_cells), NN)
        gathered_ref[:, pl.ds(start, span)] = pick_group(
            gathered, cell // low_cells, cycles
        ).astype(BF16)


def backward_kernel(
    span,
    tile_rows,
    frame_ref,
    from_west_ref,
    from_east_ref,
    latent_ref,
    cell_ref,
    pixel_ref,
    weight_ref,
    row_latent_ref,
    share_ref,
    totals_ref,
    part_ref,
    misfit,
):
    cycles, low_cells, width = latent_ref.shape
    early = row_latent_ref.shape[1]
    frame_rows, frame_width = frame_ref.shape
    variables = frame_rows // tile_rows
    half = frame_width // 2
    misfit[:, :half] = (frame_ref[:, :half] + from_west_ref[...].astype(F32)).astype(BF16)
    misfit[:, half:] = (frame_ref[:, half:] + from_east_ref[...].astype(F32)).astype(BF16)
    head_part = jnp.zeros((variables, width), F32)
    bias_part = jnp.zeros((variables, 128), F32)
    totals_ref[...] = jnp.zeros_like(totals_ref)
    for start in reversed(range(0, pixel_ref.shape[1], span)):
        pixel = pixel_ref[:, pl.ds(start, span)]
        gathered = dot(misfit[...], low_one_hot(pixel, frame_width), NN)
        share = (
            pick_group(gathered, pixel // frame_width, tile_rows)
            * weight_ref[:, pl.ds(start, span)]
        )
        for lane in range(0, span, 128):
            bias_part += share[:, lane : lane + 128]
        if start < early:
            narrow = share.astype(BF16)
            share_ref[:, pl.ds(start, span)] = narrow
        else:
            cell = cell_ref[:, pl.ds(start, span)]
            totals_ref[...] += dot(
                spread_groups(share, cell // low_cells, cycles), low_one_hot(cell, low_cells), NT
            )
    for c in range(cycles):
        rows = slice(c * variables, (c + 1) * variables)
        head_part += dot(totals_ref[rows, :].astype(BF16), latent_ref[c], NN)
    head_part += dot(share_ref[...], row_latent_ref[...], NT)
    part_ref[...] = jnp.zeros_like(part_ref)
    part_ref[:variables, :] = head_part
    part_ref[variables : variables + 1, :variables] = jnp.sum(
        jnp.where(eye(variables), jnp.sum(bias_part, axis=1, keepdims=True), 0.0),
        axis=0,
        keepdims=True,
    )


def cell_kernel(span, share_ref, cell_ref, late_ref, cell_misfit_ref, totals):
    variables, early = share_ref.shape
    groups, low_cells = totals.shape[0] // variables, totals.shape[1]
    totals[...] = late_ref[...]
    for start in range(0, early, span):
        cell = cell_ref[:, pl.ds(start, span)]
        totals[...] += dot(
            spread_groups(share_ref[:, pl.ds(start, span)], cell // low_cells, groups),
            low_one_hot(cell, low_cells),
            NT,
        )
    cell_misfit_ref[...] = totals[...].astype(BF16)


def latent_kernel(cell_misfit_ref, head_ref, latent_grad_ref):
    variables = head_ref.shape[0]
    for c in range(latent_grad_ref.shape[0]):
        rows = slice(c * variables, (c + 1) * variables)
        wide = cell_misfit_ref[rows, :].astype(F32)
        latent_grad_ref[c] = dot(wide.T.astype(BF16), head_ref[...], NN).astype(BF16)


def finish_kernel(scale, mine_ref, theirs_ref, head_grad_ref, bias_grad_ref):
    variables = head_grad_ref.shape[0]
    head_grad_ref[...] = (mine_ref[:variables, :] + theirs_ref[:variables, :]) * scale
    last = slice(variables, variables + 1)
    bias_grad_ref[...] = (mine_ref[last, :variables] + theirs_ref[last, :variables]) * scale


def sum_rounds(lat, lon):
    rounds = []
    low_first = [1 << k for k in range(lat.bit_length() - 1)]
    while low_first:
        pair, low_first = low_first[:2], low_first[2:]
        flips = pair + [pair[0] ^ pair[-1]] * (len(pair) - 1)
        rounds.append([(s, 0) for s in flips[1:] + flips[:1]])
    cross = min(lat - 1, 1)
    high_first = [1 << k for k in reversed(range(lon.bit_length() - 1))]
    while high_first:
        take = 2 - len(high_first) % 2
        pair, high_first = high_first[:take], high_first[take:]
        rounds.append([(cross, s) for s in pair[:1] + [pair[0] ^ pair[-1]] * (take - 1) + pair[1:]])
    return rounds


def add_pairs(values):
    while len(values) > 1:
        values = [values[i] + values[i + 1] for i in range(0, len(values), 2)]
    return values[0]


def sum_but_last(value, jobs):
    lat, lon = lax.axis_size("lat"), lax.axis_size("lon")

    def swap(shard, flip):
        pairs = [
            (i * lon + j, (i ^ flip[0]) * lon + (j ^ flip[1])) for i in range(lat) for j in range(lon)
        ]
        return lax.ppermute(shard, ("lat", "lon"), pairs).astype(F32)

    jobs, done = list(jobs), None
    powers = lat & (lat - 1) == 0 and lon & (lon - 1) == 0
    rounds = sum_rounds(lat, lon) if powers else []
    for flips in rounds[:-1]:
        narrow = value.astype(BF16)
        shards = [narrow.astype(F32)] + [swap(narrow, flip) for flip in flips]
        if jobs:
            done = jobs.pop(0)(done)
            value, done = lax.optimization_barrier((add_pairs(shards), done))
        else:
            value = add_pairs(shards)
    for job in jobs:
        done = job(done)
    if not rounds:
        return lax.psum(value, ("lat", "lon")), jnp.zeros_like(value), done
    narrow = value.astype(BF16)
    last = [narrow.astype(F32)] + [swap(narrow, flip) for flip in rounds[-1]]
    half = len(last) // 2
    return add_pairs(last[:half]), add_pairs(last[half:]), done


def from_behind(shard, axis, by):
    devices = lax.axis_size(axis)
    return lax.ppermute(shard, axis, [(i, (i + by) % devices) for i in range(devices)])


def per_device(latent, head, bias, targets, margin_cell, margin_pixel, margin_weight, live_count):
    cycles, low_cells, width = latent.shape
    variables, tile_rows, tile_cols = targets.shape
    frame_shape = (tile_rows * variables, 2 * tile_cols)
    half_shape = (tile_rows * variables, tile_cols)
    cell_shape = (cycles * variables, low_cells)
    cell = margin_cell.reshape(1, -1)
    pixel = margin_pixel.reshape(1, -1)
    weight = margin_weight.reshape(1, -1)
    span = math.gcd(1024, cell.shape[1])
    hbm = pl.BlockSpec(memory_space=pltpu.HBM)
    vmem = pl.BlockSpec(memory_space=pltpu.VMEM)
    params = pltpu.CompilerParams(vmem_limit_bytes=24 * 1024 * 1024)
    frame, west, east, latent, head_t, cell, pixel, weight = pl.pallas_call(
        functools.partial(forward_kernel, span),
        out_shape=(
            jax.ShapeDtypeStruct(frame_shape, F32),
            jax.ShapeDtypeStruct(half_shape, BF16),
            jax.ShapeDtypeStruct(half_shape, BF16),
            jax.ShapeDtypeStruct(latent.shape, BF16),
            jax.ShapeDtypeStruct((variables, width), BF16),
            jax.ShapeDtypeStruct(cell.shape, jnp.int32),
            jax.ShapeDtypeStruct(cell.shape, jnp.int32),
            jax.ShapeDtypeStruct(cell.shape, F32),
        ),
        in_specs=[pl.BlockSpec(memory_space=pltpu.SMEM), hbm, vmem, hbm, hbm, hbm, hbm, hbm],
        out_specs=[vmem] * 8,
        scratch_shapes=[
            pltpu.VMEM((1, variables), F32),
            pltpu.VMEM(targets.shape, BF16),
            pltpu.VMEM(cell_shape, BF16),
            pltpu.VMEM((variables, tile_rows, tile_cols), F32),
            pltpu.VMEM((frame_shape[0], cell.shape[1]), BF16),
            pltpu.VMEM((frame_shape[1], cell.shape[1]), BF16),
            pltpu.SemaphoreType.DMA((6,)),
        ],
        compiler_params=params,
        name="forward",
    )(
        live_count,
        pltpu.with_memory_space_constraint(latent, pltpu.HBM),
        head.T,
        pltpu.with_memory_space_constraint(bias.reshape(1, -1), pltpu.HBM),
        pltpu.with_memory_space_constraint(targets, pltpu.HBM),
        pltpu.with_memory_space_constraint(cell, pltpu.HBM),
        pltpu.with_memory_space_constraint(pixel, pltpu.HBM),
        pltpu.with_memory_space_constraint(weight, pltpu.HBM),
    )
    from_west = from_behind(east, "lon", 1)
    from_east = from_behind(west, "lon", -1)
    row_total = cell.shape[1]
    early = row_total * 2 // 3 // span * span
    row_latent = pl.pallas_call(
        functools.partial(gather_latent_kernel, span),
        out_shape=jax.ShapeDtypeStruct((width, early), BF16),
        in_specs=[vmem, vmem],
        out_specs=vmem,
        scratch_shapes=[pltpu.VMEM((cycles * width, low_cells), BF16)],
        compiler_params=params,
        cost_estimate=pl.CostEstimate(
            flops=2 * cycles * width * low_cells * early,
            bytes_accessed=2 * width * early,
            transcendentals=0,
        ),
        name="gather_latent",
    )(latent, cell)
    share, totals, part = pl.pallas_call(
        functools.partial(backward_kernel, span, tile_rows),
        out_shape=(
            jax.ShapeDtypeStruct((variables, early), BF16),
            jax.ShapeDtypeStruct(cell_shape, F32),
            jax.ShapeDtypeStruct((variables + 8, width), F32),
        ),
        in_specs=[vmem] * 8,
        out_specs=(vmem, vmem, vmem),
        scratch_shapes=[pltpu.VMEM(frame_shape, BF16)],
        compiler_params=params,
        name="backward",
    )(frame, from_west, from_east, latent, cell, pixel, weight, row_latent)

    def add_early_cells(_):
        return pl.pallas_call(
            functools.partial(cell_kernel, span),
            out_shape=jax.ShapeDtypeStruct(cell_shape, BF16),
            in_specs=[vmem] * 3,
            out_specs=vmem,
            scratch_shapes=[pltpu.VMEM(cell_shape, F32)],
            compiler_params=params,
            cost_estimate=pl.CostEstimate(
                flops=2 * cycles * variables * low_cells * row_total,
                bytes_accessed=2 * variables * row_total,
                transcendentals=0,
            ),
            name="cells",
        )(share, cell, totals)

    def grad_of_latent(cell_misfit):
        return pl.pallas_call(
            latent_kernel,
            out_shape=jax.ShapeDtypeStruct(latent.shape, BF16),
            in_specs=[vmem, vmem],
            out_specs=vmem,
            compiler_params=params,
            cost_estimate=pl.CostEstimate(
                flops=2 * cycles * low_cells * width * variables,
                bytes_accessed=2 * cycles * low_cells * width,
                transcendentals=0,
            ),
            name="latent_gradient",
        )(cell_misfit, head_t)

    mine, theirs, latent_grad = sum_but_last(part, (add_early_cells, grad_of_latent))
    cell_total = cycles * low_cells * lax.axis_size("lat") * lax.axis_size("lon")
    head_grad, bias_grad = pl.pallas_call(
        functools.partial(finish_kernel, 1.0 / math.sqrt(cell_total)),
        out_shape=(
            jax.ShapeDtypeStruct((variables, width), F32),
            jax.ShapeDtypeStruct((1, variables), F32),
        ),
        in_specs=[vmem, vmem],
        out_specs=(vmem, vmem),
        compiler_params=pltpu.CompilerParams(vmem_limit_bytes=1024 * 1024),
        name="finish",
    )(mine, theirs)
    return latent_grad, head_grad.T, bias_grad.reshape(variables)


def solution(mesh):
    in_specs = (
        P("lat", "lon", None),
        P(),
        P(),
        P(None, "lat", "lon"),
        P("lat", "lon", None),
        P("lat", "lon", None),
        P("lat", "lon", None),
        P("lat", "lon"),
    )
    out_specs = (P("lat", "lon", None), P(), P())
    return jax.shard_map(
        per_device, mesh=mesh, in_specs=in_specs, out_specs=out_specs, check_vma=False
    )
```
